256 devices in a mesh: row: 32 (over x, z), col: 8 (over y, core).
Axes of the slice: x: 4, y: 4, z: 8, core: 2. Of those that a mesh axis runs over, the one named last changes fastest.
Arguments:
- kept_tiles: int32 [32, 8, 2, 2], replicated, may hold values from -1 to 127, as said below
- density: bfloat16 [32, 8, 2, 256, 256], P('row', 'col'), may hold values from -6 to 6
Outputs:
- square: bfloat16 [32, 8, 2, 256, 256], P('row', 'col')
- updated: bfloat16 [32, 8, 2, 256, 256], P('row', 'col')
The draws below stay inside these ranges and needn't reach their ends.
Inputs may be any that keep to these rules, and one draw needn't show every extreme that they name: `kept_tiles`: A slot holds a tile row and a tile column, both -1 for an empty slot. Every tile is listed at most once. The 128 tile rows are split into 32 groups of 4, the 128 tile columns into 8 groups of 16; a tile lies on the device of its row's group and its column's group. A tile row holds at most 7 tiles. Some device fills all 2 slots.
All inputs are finite; a program needn't handle non-finite values.
Results may differ from the reference program's by a relative error of at most 0.0013.
Values may be sent and summed in bfloat16 or wider, within the bound.
No kernel may reach another device: no remote copies, remote signals or barrier semaphores. Data moves between devices by JAX's collectives and lax.ppermute only.
A program may use at most 128 MiB of HBM per device.

```python
import jax
import jax.numpy as jnp
from jax import lax

TILE = 256
BAND = 5
TR = 4
CAP = 2
N_ROW = 32
N_COL = 8


def draw_kept_tiles(key, part):
    key = jax.random.fold_in(key, 11)
    key_rows, key_cols, key_pick, key_noise = jax.random.split(key, 4)
    size = TR * N_ROW
    width = size // N_COL
    cells = TR * width
    reach = (BAND - 1) // 2
    row_perm = jax.random.permutation(key_rows, size).astype(jnp.int32)
    col_perm = jax.random.permutation(key_cols, size).astype(jnp.int32)
    group_rows = row_perm.reshape(N_ROW, TR)
    group_cols = col_perm.reshape(N_COL, width)
    cell_row = jnp.broadcast_to(group_rows[:, None, :, None], (N_ROW, N_COL, TR, width)).reshape(N_ROW, N_COL, cells)
    cell_col = jnp.broadcast_to(group_cols[None, :, None, :], (N_ROW, N_COL, TR, width)).reshape(N_ROW, N_COL, cells)
    offset = jnp.mod(cell_col - cell_row + reach, size)
    band = offset <= 2 * reach
    chosen = jax.random.randint(key_pick, (), 0, N_ROW * N_COL)
    device_ids = jnp.arange(N_ROW * N_COL, dtype=jnp.int32).reshape(N_ROW, N_COL, 1)
    eligible = band | (device_ids == chosen)
    noise = jax.random.randint(key_noise, (N_ROW, N_COL, cells), 0, 1 << 20)
    cell_ids = jnp.arange(cells, dtype=jnp.int32)
    score = eligible.astype(jnp.int32) * (1 << 28) + band.astype(jnp.int32) * (1 << 27) + noise * 64 + cell_ids
    order = jnp.argsort(-score, axis=-1)[:, :, :CAP]
    taken = jnp.take_along_axis(eligible, order, axis=-1)
    pick_row = jnp.where(taken, jnp.take_along_axis(cell_row, order, axis=-1), -1)
    pick_col = jnp.where(taken, jnp.take_along_axis(cell_col, order, axis=-1), -1)
    return jnp.stack([pick_row, pick_col], axis=2).astype(jnp.int32)


def shard_levels(rng, shape, cuts, low, largest):
    def one(dim, blocks):
        steps = jax.random.uniform(jax.random.fold_in(jax.random.fold_in(rng, 6), dim), (blocks,), jnp.float32, low / len(cuts), largest / len(cuts))
        return jnp.repeat(jnp.exp(steps), shape[dim] // blocks).reshape((-1,) + (1,) * (len(shape) - dim - 1))

    factor_of = one(*cuts[0])
    for cut in cuts[1:]:
        factor_of = factor_of * one(*cut)
    return factor_of


def centred(own_key, extent, deviation, most, shards=(), kind=jnp.bfloat16):
    entries = deviation * jax.random.normal(own_key, extent, jnp.float32)
    if shards:
        entries = entries * shard_levels(own_key, extent, shards, -0.22, 0.18)
    return jnp.clip(entries, -most, most).astype(kind)


def setup_inputs(seed: int = 0) -> dict:
    arg_keys = jax.random.split(jax.random.key(seed), 3)
    return {
        "kept_tiles": draw_kept_tiles(jax.random.fold_in(arg_keys[2], 71), 0),
        "density": centred(arg_keys[1], (N_ROW, N_COL, CAP, TILE, TILE), 1.0, 6.0, ((0, 32), (1, 8))),
    }


def tile_maps(rows, cols, live):
    count = rows.shape[0]
    size = TR * N_ROW
    put_row = jnp.where(live, rows, size)
    put_col = jnp.where(live, cols, size)
    index = jnp.full((size + 1, size + 1), count, jnp.int32)
    index = index.at[put_row, put_col].set(jnp.arange(count, dtype=jnp.int32))
    index = index[:size, :size]
    column_ids = jnp.arange(size, dtype=jnp.int32)
    score = jnp.where(index < count, column_ids[None, :], size + column_ids[None, :])
    row_cols = jnp.argsort(score, axis=1)[:, :BAND + CAP].astype(jnp.int32)
    return (index, row_cols)

def filtered_product(left, right, rows, cols, index, row_cols):
    safe_rows = jnp.maximum(rows, 0)
    safe_cols = jnp.maximum(cols, 0)

    def one(entry):
        i = safe_rows[entry]
        j = safe_cols[entry]
        middle = row_cols[i]
        first = index[i, middle]
        second = index[middle, j]
        return jnp.einsum('sij,sjk->ik', left[first].astype(jnp.float32), right[second].astype(jnp.float32))
    return lax.map(one, jnp.arange(rows.shape[0], dtype=jnp.int32))

def reference(kept_tiles, density):
    rows = kept_tiles[:, :, 0, :].reshape(-1)
    cols = kept_tiles[:, :, 1, :].reshape(-1)
    live = rows >= 0
    values = density.reshape(-1, TILE, TILE)
    blank = jnp.zeros((1, TILE, TILE), jnp.bfloat16)
    index, row_cols = tile_maps(rows, cols, live)
    mask = live[:, None, None]
    ssq = jnp.sum(jnp.where(mask, jnp.square(values.astype(jnp.float32)), 0.0))
    scale = 2.0 * jnp.sqrt(ssq / (TR * N_ROW * TILE))
    left = jnp.concatenate([values, blank], axis=0)
    product = filtered_product(left, left, rows, cols, index, row_cols)
    square = jnp.where(mask, product / scale, 0.0).astype(jnp.bfloat16)
    right = jnp.concatenate([square, blank], axis=0)
    second = filtered_product(left, right, rows, cols, index, row_cols)
    updated = jnp.where(mask, 1.5 * values.astype(jnp.float32) - 0.5 * second / scale, 0.0).astype(jnp.bfloat16)
    return (square.reshape(density.shape), updated.reshape(density.shape))
```

```python
import functools

import jax
import jax.numpy as jnp
from jax import lax
from jax.experimental import pallas as pl
from jax.experimental.pallas import tpu as pltpu
from jax.sharding import PartitionSpec as P

TR = 4
ROW_TILES = 7
PIECE_ROWS = 16
LANES = 128

VMEM = pltpu.VMEM
SMEM = pltpu.SMEM


def cut(tile, piece):
    bands = tile // PIECE_ROWS
    half, band = divmod(piece, bands)
    return (
        slice(band * PIECE_ROWS, (band + 1) * PIECE_ROWS),
        slice(half * LANES, (half + 1) * LANES),
    )


def prepare_kernel(live_ref, x_ref, pieces_ref, ssq_ref):
    slots, tile, _ = x_ref.shape
    n_pieces = pieces_ref.shape[0]
    total = jnp.zeros((8, tile), jnp.float32)
    for s in range(slots):
        for p in range(n_pieces):
            rows, columns = cut(tile, p)
            pieces_ref[p, s] = x_ref[s, rows, columns]
        values = x_ref[s].astype(jnp.float32)
        part = jnp.sum((values * values).reshape(tile // 8, 8, tile), axis=0)
        total += jnp.where(live_ref[s] > 0, part, 0.0)
    ssq_ref[...] = jnp.full(ssq_ref.shape, jnp.sum(total), jnp.float32)


def select_kernel(pick_ref, held_ref, out_ref):
    n_to, capacity = out_ref.shape[:2]

    def body(d, _):
        for q in range(capacity):
            out_ref[d, q] = held_ref[pick_ref[d, q]]
        return 0

    lax.fori_loop(0, n_to, body, 0)


def whole(ref, q, tile):
    n_pieces = ref.shape[0]
    halves = tile // LANES
    bands = n_pieces // halves
    parts = [ref[h * bands:(h + 1) * bands, q].reshape(tile, LANES) for h in range(halves)]
    return jnp.concatenate(parts, axis=1)


def accumulate(left_ref, panel_ref, received_ref, local_right, total_ref, tile):
    slots = total_ref.shape[0]
    capacity = received_ref.shape[1]
    total_ref[...] = jnp.zeros_like(total_ref)

    def add(u, index, right):
        @pl.when(index >= 0)
        def _():
            total_ref[u] += jnp.dot(
                panel_ref[jnp.maximum(index, 0)], right(), preferred_element_type=jnp.float32
            )

    for u in range(slots):
        for v in range(slots):
            add(u, left_ref[u, v], functools.partial(local_right, v))
        for q in range(capacity):
            add(u, left_ref[u, slots + q], functools.partial(whole, received_ref, q, tile))


def first_kernel(left_ref, panel_ref, received_ref, x_ref, pieces_ref, total_ref):
    slots, tile, _ = x_ref.shape
    accumulate(left_ref, panel_ref, received_ref, lambda v: x_ref[v], total_ref, tile)
    for s in range(slots):
        for p in range(pieces_ref.shape[0]):
            rows, columns = cut(tile, p)
            pieces_ref[p, s] = total_ref[s, rows, columns].astype(jnp.bfloat16)


def second_kernel(order, left_ref, live_ref, panel_ref, received_ref, x_ref, product_ref, ssq_ref,
                  square_ref, updated_ref, total_ref):
    slots, tile, _ = x_ref.shape
    accumulate(left_ref, panel_ref, received_ref,
               lambda v: product_ref[v].astype(jnp.bfloat16), total_ref, tile)
    sums = jnp.sum(ssq_ref[...], axis=0, keepdims=True)
    scale = 2.0 * jnp.sqrt(sums / order)
    scale = jnp.concatenate([scale] * (tile // LANES), axis=1)
    for s in range(slots):
        live = live_ref[s] > 0
        square_ref[s] = jnp.where(live, product_ref[s] / scale, 0.0).astype(jnp.bfloat16)
        second = total_ref[s] / scale
        updated = 1.5 * x_ref[s].astype(jnp.float32) - 0.5 * second / scale
        updated_ref[s] = jnp.where(live, updated, 0.0).astype(jnp.bfloat16)


def kernel_call(body, outs, ins, scratch=(), flops=0, touched=0):
    return pl.pallas_call(
        body,
        out_shape=outs,
        in_specs=[pl.BlockSpec(memory_space=space) for space, _ in ins],
        out_specs=[pl.BlockSpec(memory_space=VMEM) for _ in outs],
        scratch_shapes=list(scratch),
        compiler_params=pltpu.CompilerParams(vmem_limit_bytes=40 * 1024 * 1024),
        cost_estimate=pl.CostEstimate(flops=flops, bytes_accessed=touched, transcendentals=0),
    )(*[value for _, value in ins])


def plan(kept_tiles, row_id, col_id, most):
    n_row, n_col, _, slots = kept_tiles.shape
    size = n_row * TR
    held = n_row * slots
    rows = kept_tiles[:, :, 0, :].transpose(1, 0, 2).reshape(n_col, held)
    cols = kept_tiles[:, :, 1, :].transpose(1, 0, 2).reshape(n_col, held)
    ids = jnp.arange(size, dtype=jnp.int32)
    hot_rows = (rows[:, :, None] == ids).astype(jnp.bfloat16)
    hot_cols = (cols[:, :, None] == ids).astype(jnp.bfloat16)
    pattern = jnp.einsum("gsi,gsk->ik", hot_rows, hot_cols).astype(jnp.bfloat16)
    reach = jnp.einsum("gti,ik->gtk", hot_rows, pattern).astype(jnp.bfloat16)
    meet = jnp.einsum("gtk,gsk->gts", reach, hot_rows)
    need = (meet > 0) & (cols[:, :, None] == cols[:, None, :])
    place = jnp.arange(held, dtype=jnp.int32)
    devices = jnp.arange(n_row, dtype=jnp.int32)
    remote = devices[:, None] != place[None, :] // slots
    wanted = need.reshape(n_col, n_row, slots, held).any(2) & remote
    largest = jnp.max(jnp.sum(wanted.astype(jnp.int32), axis=-1))

    mine = lax.dynamic_index_in_dim(wanted, col_id, 0, False)
    before = (place[:, None] < place[None, :]).astype(jnp.bfloat16)
    rank = jnp.dot(mine.astype(jnp.bfloat16), before, preferred_element_type=jnp.float32)
    turn = jnp.arange(most, dtype=jnp.int32)
    chosen = mine[:, None, :] & (rank.astype(jnp.int32)[:, None, :] == turn[None, :, None])
    pick = jnp.sum(jnp.where(chosen, place, 0), axis=-1)

    own_rows = lax.dynamic_index_in_dim(rows, col_id, 0, False)
    own_need = lax.dynamic_index_in_dim(need, col_id, 0, False)
    first = row_id * slots
    own_need = lax.dynamic_slice_in_dim(own_need, first, slots, 0)
    target = lax.dynamic_slice_in_dim(own_rows, first, slots, 0)
    panel = lax.dynamic_index_in_dim(kept_tiles, row_id, 0, False)
    panel_rows = panel[:, 0, :].reshape(-1)
    panel_cols = panel[:, 1, :].reshape(-1)
    same = (panel_rows == target[:, None, None]) & (panel_cols == own_rows[None, :, None])
    spot = jnp.arange(n_col * slots, dtype=jnp.int32)
    left = jnp.where(own_need, jnp.sum(jnp.where(same, spot, 0), axis=-1), -1)
    own_chosen = lax.dynamic_index_in_dim(chosen, row_id, 0, False)
    far = jnp.sum(jnp.where(own_chosen[None], left[:, None, :] + 1, 0), axis=-1) - 1
    near = lax.dynamic_slice_in_dim(left, first, slots, 1)
    live = (target >= 0).astype(jnp.int32)
    return largest, pick, jnp.concatenate([near, far], axis=1), live


def local(kept_tiles, density):
    row_id = lax.axis_index("row")
    col_id = lax.axis_index("col")
    n_row, n_col, _, slots = kept_tiles.shape
    tile = density.shape[-1]
    order = n_row * TR * tile
    most = slots * ROW_TILES
    mine = density.reshape(slots, tile, tile)
    own = lax.dynamic_index_in_dim(lax.dynamic_index_in_dim(kept_tiles, row_id, 0, False), col_id, 0, False)
    own_live = (own[0] >= 0).astype(jnp.int32)
    piece = (PIECE_ROWS, LANES)
    spread = jax.ShapeDtypeStruct((n_row, slots) + piece, jnp.bfloat16)

    pieces, ssq = kernel_call(
        prepare_kernel,
        [spread, jax.ShapeDtypeStruct((1, LANES), jnp.float32)],
        [(SMEM, own_live), (VMEM, mine)],
        touched=4 * mine.size,
    )

    def exchange(x):
        return lax.all_to_all(x, "row", 0, 0, tiled=True)

    held = exchange(pieces)
    largest, pick, left, live = plan(kept_tiles, row_id, col_id, most)

    def route(held, pick, capacity):
        out = jax.ShapeDtypeStruct((n_row, capacity) + piece, jnp.bfloat16)
        (sent,) = kernel_call(
            select_kernel, [out],
            [(SMEM, pick[:, :capacity]), (VMEM, held.reshape((n_row * slots,) + piece))],
            touched=n_row * capacity * PIECE_ROWS * LANES * 4,
        )
        return exchange(sent)

    def finish(capacity, mine, held, ssq, pick, left, live):
        left = left[:, :slots + capacity]
        panel = lax.all_gather(mine, "col", axis=0, tiled=True)
        sums = lax.all_gather(ssq, ("row", "col"), axis=0, tiled=True)
        received = route(held, pick, capacity)
        full = jax.ShapeDtypeStruct((slots, tile, tile), jnp.float32)
        out = jax.ShapeDtypeStruct((slots, tile, tile), jnp.bfloat16)
        work = 4 * 2 * tile ** 3
        pieces, product = kernel_call(
            first_kernel, [spread, full],
            [(SMEM, left), (VMEM, panel), (VMEM, received), (VMEM, mine)],
            flops=work, touched=2 * panel.size,
        )
        received = route(exchange(pieces), pick, capacity)
        square, updated = kernel_call(
            functools.partial(second_kernel, order), [out, out],
            [(SMEM, left), (SMEM, live), (VMEM, panel), (VMEM, received), (VMEM, mine),
             (VMEM, product), (VMEM, sums)],
            scratch=[VMEM((slots, tile, tile), jnp.float32)],
            flops=work, touched=2 * panel.size,
        )
        return square, updated

    capacities = sorted({min(c, most) for c in (6, 7, 8, most)})
    branch = sum((largest > c).astype(jnp.int32) for c in capacities[:-1])
    square, updated = lax.switch(
        branch, [functools.partial(finish, c) for c in capacities],
        mine, held, ssq, pick, left, live,
    )
    return square.reshape(density.shape), updated.reshape(density.shape)


def solution(mesh):
    spec = P("row", "col", None, None, None)
    return jax.shard_map(local, mesh=mesh, in_specs=(P(), spec), out_specs=(spec, spec), check_vma=False)
```

```python
import functools

import jax
import jax.numpy as jnp
from jax import lax
from jax.experimental import pallas as pl
from jax.experimental.pallas import tpu as pltpu
from jax.sharding import PartitionSpec as P

TR = 4
ROW_TILES = 7
BLOCK = (16, 128)
PARTS = 3

VMEM = pltpu.VMEM
SMEM = pltpu.SMEM
F32 = jnp.float32
BF16 = jnp.bfloat16


def cut(tile, piece):
    rows, lanes = BLOCK
    half, band = divmod(piece, tile // rows)
    return slice(band * rows, (band + 1) * rows), slice(half * lanes, (half + 1) * lanes)


def whole(ref, q, tile):
    rows, lanes = BLOCK
    bands = tile // rows
    return jnp.concatenate(
        [ref[h * bands:(h + 1) * bands, q].reshape(tile, lanes) for h in range(tile // lanes)], axis=1
    )


def split(value, first, into):
    row = lax.broadcasted_iota(jnp.int32, BLOCK, 0)
    lane = lax.broadcasted_iota(jnp.int32, BLOCK, 1)
    rest = jnp.full(BLOCK, value, F32)
    for t in range(PARTS):
        this = rest.astype(BF16).astype(F32)
        into = jnp.where((row == 0) & (lane == first + t), this, into)
        rest = rest - this
    return into


def prepare_kernel(x_ref, out_ref):
    slots, tile, _ = x_ref.shape
    sums = jnp.zeros(BLOCK, F32)
    for s in range(slots):
        for p in range(out_ref.shape[0]):
            rows, columns = cut(tile, p)
            out_ref[p, s] = x_ref[s, rows, columns]
        value = x_ref[s].astype(F32)
        part = jnp.sum((value * value).reshape(tile // 8, 8, tile), axis=0)
        sums = split(jnp.sum(part), s * PARTS, sums)
    for p in range(out_ref.shape[0]):
        out_ref[p, slots] = sums.astype(BF16)


def select_kernel(pick_ref, held_ref, *refs):
    out_ref = refs[-1]
    n_to, capacity = out_ref.shape[:2]

    def body(d, _):
        for q in range(capacity):
            place = pick_ref[d, q]
            out_ref[d, q] = held_ref[place // 2, place % 2]
        return 0

    lax.fori_loop(0, n_to, body, 0)


def select_sum_kernel(pick_ref, held_ref, x_ref, mask_ref, panel_ref, out_ref):
    slots, tile, _ = x_ref.shape
    parts = held_ref[:, slots].astype(F32)
    total = jnp.sum(jnp.sum(parts, axis=1) * mask_ref[...])
    for s in range(slots):
        panel_ref[s * tile:(s + 1) * tile] = x_ref[s]
    sums = split(total, 0, jnp.zeros(BLOCK, F32)).astype(BF16)
    panel_ref[slots * tile:, :BLOCK[1]] = sums
    panel_ref[slots * tile:, BLOCK[1]:] = jnp.zeros((BLOCK[0], tile - BLOCK[1]), BF16)
    select_kernel(pick_ref, held_ref, out_ref)


def accumulate(left_ref, panel_ref, received_ref, own_ref, total_ref, ready=None):
    slots, tile, _ = total_ref.shape
    total_ref[...] = jnp.zeros_like(total_ref)

    def add(u, n, ref, q):
        index = left_ref[u, n]

        @pl.when(index >= 0)
        def _():
            if ready is None:
                device = index // slots
                row = pl.multiple_of(index % slots * tile, tile)
                left = panel_ref[device, pl.ds(row, tile)]
            else:
                left = ready(u, n)
            total_ref[u] += jnp.dot(left, whole(ref, q, tile), preferred_element_type=F32)

    for u in range(slots):
        for v in range(slots):
            add(u, v, own_ref, v)
        for q in range(received_ref.shape[1]):
            add(u, slots + q, received_ref, q)


def scale_of(sums, order):
    total = jnp.full((1, BLOCK[1]), jnp.sum(sums.astype(F32)), F32)
    return 2.0 * jnp.sqrt(total / order)[0:1, 0:1]


def first_kernel(order, left_ref, live_ref, panel_ref, received_ref, own_ref, pieces_ref,
                 total_ref, left_tiles, sums_ref, sems, sum_sem):
    slots, tile, _ = total_ref.shape
    turns = left_ref.shape[1]
    sums = pltpu.make_async_copy(
        panel_ref.at[:, pl.ds(slots * tile, BLOCK[0]), pl.ds(0, BLOCK[1])], sums_ref, sum_sem)

    def fetch(u, n):
        index = jnp.maximum(left_ref[u, n], 0)
        row = pl.multiple_of(index % slots * tile, tile)
        return pltpu.make_async_copy(
            panel_ref.at[index // slots, pl.ds(row, tile)], left_tiles.at[u * turns + n], sems.at[u * turns + n])

    for u in range(slots):
        for n in range(turns):
            @pl.when(left_ref[u, n] >= 0)
            def _():
                fetch(u, n).start()
    sums.start()

    def ready(u, n):
        fetch(u, n).wait()
        return left_tiles[u * turns + n]

    accumulate(left_ref, panel_ref, received_ref, own_ref, total_ref, ready)
    sums.wait()
    scale = scale_of(sums_ref[...], order)
    for s in range(slots):
        square = jnp.where(live_ref[s] > 0, total_ref[s] / scale, 0.0).astype(BF16)
        for p in range(pieces_ref.shape[0]):
            rows, columns = cut(tile, p)
            pieces_ref[p, s] = square[rows, columns]


def second_kernel(order, left_ref, live_ref, panel_ref, received_ref, own_ref, x_ref, square_ref,
                  updated_ref, total_ref):
    slots, tile, _ = total_ref.shape
    accumulate(left_ref, panel_ref, received_ref, own_ref, total_ref)
    scale = scale_of(panel_ref[:, slots * tile:, :BLOCK[1]], order)
    for s in range(slots):
        new = 1.5 * x_ref[s].astype(F32) - 0.5 * total_ref[s] / scale
        updated_ref[s] = jnp.where(live_ref[s] > 0, new, 0.0).astype(BF16)
        square_ref[s] = whole(own_ref, s, tile)


def kernel_call(body, outs, ins, scratch=(), flops=0, touched=0):
    return pl.pallas_call(
        body,
        out_shape=outs,
        in_specs=[pl.BlockSpec(memory_space=space) for space, _ in ins],
        out_specs=[pl.BlockSpec(memory_space=VMEM) for _ in outs],
        scratch_shapes=list(scratch),
        compiler_params=pltpu.CompilerParams(vmem_limit_bytes=40 * 1024 * 1024),
        cost_estimate=pl.CostEstimate(flops=flops, bytes_accessed=touched, transcendentals=0),
    )(*[value for _, value in ins])


def plan(kept_tiles, row_id, col_id, most):
    n_row, n_col, _, slots = kept_tiles.shape
    size = n_row * TR
    held = n_row * slots
    rows = kept_tiles[:, :, 0, :].transpose(1, 0, 2).reshape(n_col, held)
    cols = kept_tiles[:, :, 1, :].transpose(1, 0, 2).reshape(n_col, held)
    ids = jnp.arange(size, dtype=jnp.int32)
    hot_rows = (rows[:, :, None] == ids).astype(jnp.bfloat16)
    hot_cols = (cols[:, :, None] == ids).astype(jnp.bfloat16)
    pattern = jnp.einsum("gsi,gsk->ik", hot_rows, hot_cols).astype(jnp.bfloat16)
    reach = jnp.einsum("gti,ik->gtk", hot_rows, pattern).astype(jnp.bfloat16)
    meet = jnp.einsum("gtk,gsk->gts", reach, hot_rows)
    need = (meet > 0) & (cols[:, :, None] == cols[:, None, :])
    place = jnp.arange(held, dtype=jnp.int32)
    devices = jnp.arange(n_row, dtype=jnp.int32)
    remote = devices[:, None] != place[None, :] // slots
    wanted = need.reshape(n_col, n_row, slots, held).any(2) & remote
    largest = jnp.max(jnp.sum(wanted.astype(jnp.int32), axis=-1))

    mine = lax.dynamic_index_in_dim(wanted, col_id, 0, False)
    before = (place[:, None] < place[None, :]).astype(jnp.bfloat16)
    rank = jnp.dot(mine.astype(jnp.bfloat16), before, preferred_element_type=jnp.float32)
    turn = jnp.arange(most, dtype=jnp.int32)
    chosen = mine[:, None, :] & (rank.astype(jnp.int32)[:, None, :] == turn[None, :, None])
    pick = jnp.sum(jnp.where(chosen, place, 0), axis=-1)

    own_rows = lax.dynamic_index_in_dim(rows, col_id, 0, False)
    own_need = lax.dynamic_index_in_dim(need, col_id, 0, False)
    first = row_id * slots
    own_need = lax.dynamic_slice_in_dim(own_need, first, slots, 0)
    target = lax.dynamic_slice_in_dim(own_rows, first, slots, 0)
    panel = lax.dynamic_index_in_dim(kept_tiles, row_id, 0, False)
    panel_rows = panel[:, 0, :].reshape(-1)
    panel_cols = panel[:, 1, :].reshape(-1)
    same = (panel_rows == target[:, None, None]) & (panel_cols == own_rows[None, :, None])
    spot = jnp.arange(n_col * slots, dtype=jnp.int32)
    left = jnp.where(own_need, jnp.sum(jnp.where(same, spot, 0), axis=-1), -1)
    own_chosen = lax.dynamic_index_in_dim(chosen, row_id, 0, False)
    far = jnp.sum(jnp.where(own_chosen[None], left[:, None, :] + 1, 0), axis=-1) - 1
    near = lax.dynamic_slice_in_dim(left, first, slots, 1)
    live = (target >= 0).astype(jnp.int32)
    return largest, pick, jnp.concatenate([near, far], axis=1), live


def local(kept_tiles, density):
    row_id = lax.axis_index("row")
    col_id = lax.axis_index("col")
    n_row, n_col, _, slots = kept_tiles.shape
    tile = density.shape[-1]
    order = n_row * TR * tile
    most = slots * ROW_TILES
    mine = density.reshape(slots, tile, tile)

    def pieces_of(n):
        return jax.ShapeDtypeStruct((n_row, n) + BLOCK, BF16)

    def exchange(x):
        return lax.all_to_all(x, "row", 0, 0, tiled=True)

    (pieces,) = kernel_call(prepare_kernel, [pieces_of(slots + 1)], [(VMEM, mine)], touched=4 * mine.size)
    held = exchange(pieces)
    largest, pick, left, live = plan(kept_tiles, row_id, col_id, most)
    col_live = lax.dynamic_index_in_dim(kept_tiles, col_id, 1, False)[:, 0, :] >= 0
    lanes = jnp.arange(BLOCK[1], dtype=jnp.int32) // PARTS
    mask = sum(((lanes == s) & col_live[:, s:s + 1]).astype(F32) for s in range(slots))

    def finish(capacity, mine, pieces, held, mask, pick, left, live):
        left = left[:, :slots + capacity]
        pick = pick[:, :capacity]
        turns = left.shape[1]
        scratch = [VMEM((slots, tile, tile), F32)]
        work = 4 * 2 * tile ** 3
        moved = n_row * capacity * BLOCK[0] * BLOCK[1] * 4
        share = jax.ShapeDtypeStruct((slots * tile + BLOCK[0], tile), BF16)
        share, sent = kernel_call(
            select_sum_kernel, [share, pieces_of(capacity)],
            [(SMEM, pick), (VMEM, held), (VMEM, mine), (VMEM, mask)], touched=moved + 4 * mine.size,
        )
        panel = lax.all_gather(share, "col", axis=0, tiled=False)
        received = exchange(sent)
        (square,) = kernel_call(
            functools.partial(first_kernel, order), [pieces_of(slots)],
            [(SMEM, left), (SMEM, live), (pl.ANY, panel), (VMEM, received), (VMEM, pieces)],
            scratch=scratch + [
                VMEM((slots * turns, tile, tile), BF16), VMEM((n_col,) + BLOCK, BF16),
                pltpu.SemaphoreType.DMA((slots * turns,)), pltpu.SemaphoreType.DMA,
            ],
            flops=work, touched=panel.size,
        )
        (sent,) = kernel_call(
            select_kernel, [pieces_of(capacity)], [(SMEM, pick), (VMEM, exchange(square))], touched=moved
        )
        received = exchange(sent)
        out = jax.ShapeDtypeStruct((slots, tile, tile), BF16)
        return kernel_call(
            functools.partial(second_kernel, order), [out, out],
            [(SMEM, left), (SMEM, live), (VMEM, panel), (VMEM, received), (VMEM, square), (VMEM, mine)],
            scratch=scratch, flops=work, touched=2 * panel.size,
        )

    capacities = sorted({min(c, most) for c in (5, 6, 7, 8, most)})
    branch = sum((largest > c).astype(jnp.int32) for c in capacities[:-1])
    square, updated = lax.switch(
        branch, [functools.partial(finish, c) for c in capacities],
        mine, pieces, held, mask, pick, left, live,
    )
    return square.reshape(density.shape), updated.reshape(density.shape)


def solution(mesh):
    spec = P("row", "col", None, None, None)
    return jax.shard_map(local, mesh=mesh, in_specs=(P(), spec), out_specs=(spec, spec), check_vma=False)
```

```python
import functools

import jax
import jax.numpy as jnp
from jax import lax
from jax.experimental import pallas as pl
from jax.experimental.pallas import tpu as pltpu
from jax.sharding import PartitionSpec as P

TR = 4
ROW_TILES = 7
BLOCK = (16, 128)
EXTRA = 8
PARTS = 3
TOGETHER = 4

VMEM = pltpu.VMEM
SMEM = pltpu.SMEM
F32 = jnp.float32
BF16 = jnp.bfloat16


def cut(tile, piece):
    rows, lanes = BLOCK
    half, band = divmod(piece, tile // rows)
    return slice(band * rows, (band + 1) * rows), slice(half * lanes, (half + 1) * lanes)


def whole(ref, q, tile):
    rows, lanes = BLOCK
    bands = tile // rows
    return jnp.concatenate(
        [ref[h * bands:(h + 1) * bands, q].reshape(tile, lanes) for h in range(tile // lanes)], axis=1
    )


def split(value, first, into):
    row = lax.broadcasted_iota(jnp.int32, into.shape, 0)
    lane = lax.broadcasted_iota(jnp.int32, into.shape, 1)
    rest = jnp.full(into.shape, value, F32)
    for t in range(PARTS):
        this = rest.astype(BF16).astype(F32)
        into = jnp.where((row == 0) & (lane == first + t), this, into)
        rest = rest - this
    return into


def prepare_kernel(x_ref, out_ref):
    slots, tile, _ = x_ref.shape
    rows = BLOCK[0]
    sums = jnp.zeros((EXTRA, BLOCK[1]), F32)
    for s in range(slots):
        for p in range(out_ref.shape[0]):
            from_rows, columns = cut(tile, p)
            out_ref[p, s * rows:(s + 1) * rows] = x_ref[s, from_rows, columns]
        value = x_ref[s].astype(F32)
        part = jnp.sum((value * value).reshape(tile // 8, 8, tile), axis=0)
        sums = split(jnp.sum(part), s * PARTS, sums)
    for p in range(out_ref.shape[0]):
        out_ref[p, slots * rows:] = sums.astype(BF16)


def select(pick_ref, fetch, out_ref):
    n_to, capacity = out_ref.shape[:2]

    def body(n, _):
        spots = [(n * TOGETHER + d, q) for d in range(TOGETHER) for q in range(capacity)]
        values = [fetch(pick_ref[d, q]) for d, q in spots]
        for (d, q), value in zip(spots, values):
            out_ref[d, q] = value
        return 0

    lax.fori_loop(0, n_to // TOGETHER, body, 0)


def select_kernel(pick_ref, held_ref, out_ref):
    select(pick_ref, lambda place: held_ref[place // 2, place % 2], out_ref)


def select_first_kernel(pick_ref, held_ref, out_ref):
    rows = BLOCK[0]

    def fetch(place):
        return held_ref[place // 2, pl.ds(pl.multiple_of(place % 2 * rows, rows), rows)]

    select(pick_ref, fetch, out_ref)


def sum_kernel(held_ref, mask_ref, out_ref):
    parts = held_ref[:, held_ref.shape[1] - EXTRA:].astype(F32)
    out_ref[...] = jnp.full(out_ref.shape, jnp.sum(jnp.sum(parts, axis=1) * mask_ref[...]), F32)


def accumulate(left_ref, left_tile, received_ref, own, total_ref):
    slots, tile, _ = total_ref.shape
    capacity = received_ref.shape[1]
    total_ref[...] = jnp.zeros_like(total_ref)

    def add(u, n, right):
        @pl.when(left_ref[u, n] >= 0)
        def _():
            total_ref[u] += jnp.dot(left_tile(u, n), right(), preferred_element_type=F32)

    for u in range(slots):
        def body(q, _, u=u):
            add(u, slots + q, lambda: whole(received_ref, q, tile))
            return 0

        for v in range(slots):
            add(u, v, functools.partial(own, v))
        lax.fori_loop(0, capacity, body, 0)


def scale_of(sums_ref, order):
    return (2.0 * jnp.sqrt(sums_ref[0:1] / order))[:, 0:1]


def left_from(panel_ref, left_ref):
    def left_tile(u, n):
        return panel_ref[jnp.maximum(left_ref[u, n], 0)]

    return left_tile


def first_kernel(order, left_ref, live_ref, panel_ref, received_ref, x_ref, sums_ref, pieces_ref, total_ref):
    slots, tile, _ = total_ref.shape
    scale = scale_of(sums_ref, order)
    accumulate(left_ref, left_from(panel_ref, left_ref), received_ref, lambda v: x_ref[v], total_ref)
    for s in range(slots):
        square = jnp.where(live_ref[s] > 0, total_ref[s] / scale, 0.0).astype(BF16)
        for p in range(pieces_ref.shape[0]):
            rows, columns = cut(tile, p)
            pieces_ref[p, s] = square[rows, columns]


def second_kernel(order, left_ref, live_ref, panel_ref, received_ref, own_ref, x_ref, sums_ref,
                  square_ref, updated_ref, total_ref):
    slots, tile, _ = total_ref.shape

    scale = scale_of(sums_ref, order)
    accumulate(left_ref, left_from(panel_ref, left_ref), received_ref, lambda v: whole(own_ref, v, tile), total_ref)
    for s in range(slots):
        new = 1.5 * x_ref[s].astype(F32) - 0.5 * total_ref[s] / scale
        updated_ref[s] = jnp.where(live_ref[s] > 0, new, 0.0).astype(BF16)
        square_ref[s] = whole(own_ref, s, tile)


def kernel_call(body, outs, ins, scratch=(), flops=0, touched=0):
    return pl.pallas_call(
        body,
        out_shape=[shape for _, shape in outs],
        in_specs=[pl.BlockSpec(memory_space=space) for space, _ in ins],
        out_specs=[pl.BlockSpec(memory_space=space) for space, _ in outs],
        scratch_shapes=list(scratch),
        compiler_params=pltpu.CompilerParams(vmem_limit_bytes=40 * 1024 * 1024),
        cost_estimate=pl.CostEstimate(flops=flops, bytes_accessed=touched, transcendentals=0),
    )(*[value for _, value in ins])


def plan(kept_tiles, row_id, col_id, most):
    n_row, n_col, _, slots = kept_tiles.shape
    size = n_row * TR
    held = n_row * slots
    rows = kept_tiles[:, :, 0, :].transpose(1, 0, 2).reshape(n_col, held)
    cols = kept_tiles[:, :, 1, :].transpose(1, 0, 2).reshape(n_col, held)
    ids = jnp.arange(size, dtype=jnp.int32)
    hot_rows = (rows[:, :, None] == ids).astype(jnp.bfloat16)
    hot_cols = (cols[:, :, None] == ids).astype(jnp.bfloat16)
    pattern = jnp.einsum("gsi,gsk->ik", hot_rows, hot_cols).astype(jnp.bfloat16)
    reach = jnp.einsum("gti,ik->gtk", hot_rows, pattern).astype(jnp.bfloat16)
    meet = jnp.einsum("gtk,gsk->gts", reach, hot_rows)
    need = (meet > 0) & (cols[:, :, None] == cols[:, None, :])
    place = jnp.arange(held, dtype=jnp.int32)
    devices = jnp.arange(n_row, dtype=jnp.int32)
    remote = devices[:, None] != place[None, :] // slots
    wanted = need.reshape(n_col, n_row, slots, held).any(2) & remote
    largest = jnp.max(jnp.sum(wanted.astype(jnp.int32), axis=-1))

    mine = lax.dynamic_index_in_dim(wanted, col_id, 0, False)
    before = (place[:, None] < place[None, :]).astype(jnp.bfloat16)
    rank = jnp.dot(mine.astype(jnp.bfloat16), before, preferred_element_type=jnp.float32)
    turn = jnp.arange(most, dtype=jnp.int32)
    chosen = mine[:, None, :] & (rank.astype(jnp.int32)[:, None, :] == turn[None, :, None])
    pick = jnp.sum(jnp.where(chosen, place, 0), axis=-1)

    own_rows = lax.dynamic_index_in_dim(rows, col_id, 0, False)
    own_need = lax.dynamic_index_in_dim(need, col_id, 0, False)
    first = row_id * slots
    own_need = lax.dynamic_slice_in_dim(own_need, first, slots, 0)
    target = lax.dynamic_slice_in_dim(own_rows, first, slots, 0)
    panel = lax.dynamic_index_in_dim(kept_tiles, row_id, 0, False)
    panel_rows = panel[:, 0, :].reshape(-1)
    panel_cols = panel[:, 1, :].reshape(-1)
    same = (panel_rows == target[:, None, None]) & (panel_cols == own_rows[None, :, None])
    spot = jnp.arange(n_col * slots, dtype=jnp.int32)
    left = jnp.where(own_need, jnp.sum(jnp.where(same, spot, 0), axis=-1), -1)
    own_chosen = lax.dynamic_index_in_dim(chosen, row_id, 0, False)
    far = jnp.sum(jnp.where(own_chosen[None], left[:, None, :] + 1, 0), axis=-1) - 1
    near = lax.dynamic_slice_in_dim(left, first, slots, 1)
    live = (target >= 0).astype(jnp.int32)
    return largest, pick, jnp.concatenate([near, far], axis=1), live


def local(kept_tiles, density):
    row_id = lax.axis_index("row")
    col_id = lax.axis_index("col")
    n_row, n_col, _, slots = kept_tiles.shape
    tile = density.shape[-1]
    order = n_row * TR * tile
    most = slots * ROW_TILES
    mine = density.reshape(slots, tile, tile)

    def pieces_of(n):
        return jax.ShapeDtypeStruct((n_row, n) + BLOCK, BF16)

    def exchange(x):
        return lax.all_to_all(x, "row", 0, 0, tiled=True)

    def add_over(total, axis, inner, size):
        n = lax.axis_size(axis)

        def moved(i, by):
            place = i // inner % size
            return i + ((place + by) % size - place) * inner

        parts = [lax.ppermute(total, axis, [(i, moved(i, by)) for i in range(n)]) for by in range(1, size)]
        return sum(parts, total)

    first = jax.ShapeDtypeStruct((n_row, slots * BLOCK[0] + EXTRA, BLOCK[1]), BF16)
    (pieces,) = kernel_call(prepare_kernel, [(VMEM, first)], [(VMEM, mine)], touched=4 * mine.size)
    held = exchange(pieces)
    largest, pick, left, live = plan(kept_tiles, row_id, col_id, most)
    col_live = lax.dynamic_index_in_dim(kept_tiles, col_id, 1, False)[:, 0, :] >= 0
    lanes = jnp.arange(BLOCK[1], dtype=jnp.int32) // PARTS
    mask = sum(((lanes == s) & col_live[:, s:s + 1]).astype(F32) for s in range(slots))

    def finish(capacity, mine, held, mask, pick, left, live):
        left = left[:, :slots + capacity]
        pick = pick[:, :capacity]
        total = VMEM((slots, tile, tile), F32)
        work = 4 * 2 * tile ** 3
        moved = n_row * capacity * BLOCK[0] * BLOCK[1] * 4
        panel = lax.all_gather(mine, "col", axis=0, tiled=True)
        (sent,) = kernel_call(
            select_first_kernel, [(VMEM, pieces_of(capacity))], [(SMEM, pick), (VMEM, held)], touched=moved
        )
        (sums,) = kernel_call(
            sum_kernel, [(VMEM, jax.ShapeDtypeStruct((8, BLOCK[1]), F32))], [(VMEM, held), (VMEM, mask)]
        )
        sums = add_over(add_over(sums, "col", 2, n_col // 2), "col", 1, 2)
        received = exchange(sent)
        (square,) = kernel_call(
            functools.partial(first_kernel, order), [(VMEM, pieces_of(slots))],
            [(SMEM, left), (SMEM, live), (VMEM, panel), (VMEM, received), (VMEM, mine), (VMEM, sums)],
            scratch=[total],
            flops=work, touched=panel.size,
        )
        (sent,) = kernel_call(
            select_kernel, [(VMEM, pieces_of(capacity))], [(SMEM, pick), (VMEM, exchange(square))], touched=moved,
        )
        received = exchange(sent)
        out = jax.ShapeDtypeStruct((slots, tile, tile), BF16)
        return kernel_call(
            functools.partial(second_kernel, order), [(VMEM, out), (VMEM, out)],
            [(SMEM, left), (SMEM, live), (VMEM, panel), (VMEM, received), (VMEM, square), (VMEM, mine),
             (VMEM, sums)],
            scratch=[total], flops=work, touched=2 * panel.size,
        )

    capacities = sorted({min(c, most) for c in (5, 6, 7, 8, most)})
    branch = sum((largest > c).astype(jnp.int32) for c in capacities[:-1])
    square, updated = lax.switch(
        branch, [functools.partial(finish, c) for c in capacities],
        mine, held, mask, pick, left, live,
    )
    return square.reshape(density.shape), updated.reshape(density.shape)


def solution(mesh):
    spec = P("row", "col", None, None, None)
    return jax.shard_map(local, mesh=mesh, in_specs=(P(), spec), out_specs=(spec, spec), check_vma=False)
```

```python
import functools

import jax
import jax.numpy as jnp
from jax import lax
from jax.experimental import pallas as pl
from jax.experimental.pallas import tpu as pltpu
from jax.sharding import PartitionSpec as P

TR = 4
ROW_TILES = 7
BLOCK = (16, 128)
EXTRA = 8
PARTS = 3
TOGETHER = 4

VMEM = pltpu.VMEM
SMEM = pltpu.SMEM
F32 = jnp.float32
BF16 = jnp.bfloat16


def cut(tile, piece):
    rows, lanes = BLOCK
    half, band = divmod(piece, tile // rows)
    return slice(band * rows, (band + 1) * rows), slice(half * lanes, (half + 1) * lanes)


def whole(ref, q, tile):
    rows, lanes = BLOCK
    bands = tile // rows
    return jnp.concatenate(
        [ref[h * bands:(h + 1) * bands, q].reshape(tile, lanes) for h in range(tile // lanes)], axis=1
    )


def split(value, first, into):
    row = lax.broadcasted_iota(jnp.int32, into.shape, 0)
    lane = lax.broadcasted_iota(jnp.int32, into.shape, 1)
    rest = jnp.full(into.shape, value, F32)
    for t in range(PARTS):
        this = rest.astype(BF16).astype(F32)
        into = jnp.where((row == 0) & (lane == first + t), this, into)
        rest = rest - this
    return into


def prepare_kernel(x_ref, out_ref):
    slots, tile, _ = x_ref.shape
    rows = BLOCK[0]
    sums = jnp.zeros((EXTRA, BLOCK[1]), F32)
    for s in range(slots):
        for p in range(out_ref.shape[0]):
            from_rows, columns = cut(tile, p)
            out_ref[p, s * rows:(s + 1) * rows] = x_ref[s, from_rows, columns]
        value = x_ref[s].astype(F32)
        part = jnp.sum((value * value).reshape(tile // 8, 8, tile), axis=0)
        sums = split(jnp.sum(part), s * PARTS, sums)
    for p in range(out_ref.shape[0]):
        out_ref[p, slots * rows:] = sums.astype(BF16)


def select(pick_ref, fetch, out_ref):
    n_to, capacity = out_ref.shape[:2]

    def body(n, _):
        spots = [(n * TOGETHER + d, q) for d in range(TOGETHER) for q in range(capacity)]
        values = [fetch(pick_ref[d, q]) for d, q in spots]
        for (d, q), value in zip(spots, values):
            out_ref[d, q] = value
        return 0

    lax.fori_loop(0, n_to // TOGETHER, body, 0)


def select_kernel(pick_ref, held_ref, out_ref):
    select(pick_ref, lambda place: held_ref[place], out_ref)


def select_first_kernel(pick_ref, held_ref, out_ref):
    rows = BLOCK[0]
    select(pick_ref, lambda row: held_ref[pl.ds(pl.multiple_of(row, 8), rows)], out_ref)


def sum_kernel(held_ref, mask_ref, out_ref):
    parts = held_ref[:, held_ref.shape[1] - EXTRA:].astype(F32)
    out_ref[...] = jnp.full(out_ref.shape, jnp.sum(jnp.sum(parts, axis=1) * mask_ref[...]), F32)


def accumulate(left_ref, left_tile, received_ref, own, total_ref):
    slots, tile, _ = total_ref.shape
    capacity = received_ref.shape[1]
    total_ref[...] = jnp.zeros_like(total_ref)

    def add(u, n, right):
        @pl.when(left_ref[u, n] >= 0)
        def _():
            total_ref[u] += jnp.dot(left_tile(u, n), right(), preferred_element_type=F32)

    for u in range(slots):
        def body(q, _, u=u):
            add(u, slots + q, lambda: whole(received_ref, q, tile))
            return 0

        for v in range(slots):
            add(u, v, functools.partial(own, v))
        lax.fori_loop(0, capacity, body, 0)


def scale_of(sums_ref, order):
    return (2.0 * jnp.sqrt(sums_ref[0:1] / order))[:, 0:1]


def left_from(panel_ref, left_ref):
    def left_tile(u, n):
        return panel_ref[jnp.maximum(left_ref[u, n], 0)]

    return left_tile


def first_kernel(order, left_ref, live_ref, panel_ref, received_ref, x_ref, sums_ref, pieces_ref, total_ref):
    slots, tile, _ = total_ref.shape
    scale = scale_of(sums_ref, order)
    accumulate(left_ref, left_from(panel_ref, left_ref), received_ref, lambda v: x_ref[v], total_ref)
    for s in range(slots):
        square = jnp.where(live_ref[s] > 0, total_ref[s] / scale, 0.0).astype(BF16)
        for p in range(pieces_ref.shape[0]):
            rows, columns = cut(tile, p)
            pieces_ref[p, s] = square[rows, columns]


def second_kernel(order, left_ref, live_ref, panel_ref, received_ref, own_ref, x_ref, sums_ref,
                  square_ref, updated_ref, total_ref):
    slots, tile, _ = total_ref.shape

    scale = scale_of(sums_ref, order)
    accumulate(left_ref, left_from(panel_ref, left_ref), received_ref, lambda v: whole(own_ref, v, tile), total_ref)
    for s in range(slots):
        new = 1.5 * x_ref[s].astype(F32) - 0.5 * total_ref[s] / scale
        updated_ref[s] = jnp.where(live_ref[s] > 0, new, 0.0).astype(BF16)
        square_ref[s] = whole(own_ref, s, tile)


def kernel_call(body, outs, ins, scratch=(), flops=0, touched=0):
    return pl.pallas_call(
        body,
        out_shape=[shape for _, shape in outs],
        in_specs=[pl.BlockSpec(memory_space=space) for space, _ in ins],
        out_specs=[pl.BlockSpec(memory_space=space) for space, _ in outs],
        scratch_shapes=list(scratch),
        compiler_params=pltpu.CompilerParams(vmem_limit_bytes=40 * 1024 * 1024),
        cost_estimate=pl.CostEstimate(flops=flops, bytes_accessed=touched, transcendentals=0),
    )(*[value for _, value in ins])


def nearness(col, col_id, n_col):
    steps = (col_id // 2 - col // 2 + n_col // 2) % (n_col // 2)
    return steps * 2 + (col % 2 != col_id % 2).astype(jnp.int32)


def plan(kept_tiles, row_id, col_id, most):
    n_row, n_col, _, slots = kept_tiles.shape
    size = n_row * TR
    held = n_row * slots
    rows = kept_tiles[:, :, 0, :].transpose(1, 0, 2).reshape(n_col, held)
    cols = kept_tiles[:, :, 1, :].transpose(1, 0, 2).reshape(n_col, held)
    ids = jnp.arange(size, dtype=jnp.int32)
    hot_rows = (rows[:, :, None] == ids).astype(jnp.bfloat16)
    hot_cols = (cols[:, :, None] == ids).astype(jnp.bfloat16)
    pattern = jnp.einsum("gsi,gsk->ik", hot_rows, hot_cols).astype(jnp.bfloat16)
    reach = jnp.einsum("gti,ik->gtk", hot_rows, pattern).astype(jnp.bfloat16)
    meet = jnp.einsum("gtk,gsk->gts", reach, hot_rows)
    need = (meet > 0) & (cols[:, :, None] == cols[:, None, :])
    place = jnp.arange(held, dtype=jnp.int32)
    devices = jnp.arange(n_row, dtype=jnp.int32)
    remote = devices[:, None] != place[None, :] // slots
    wanted = need.reshape(n_col, n_row, slots, held).any(2) & remote
    largest = jnp.max(jnp.sum(wanted.astype(jnp.int32), axis=-1))

    mine = lax.dynamic_index_in_dim(wanted, col_id, 0, False)
    before = (place[:, None] < place[None, :]).astype(jnp.bfloat16)
    rank = jnp.dot(mine.astype(jnp.bfloat16), before, preferred_element_type=jnp.float32)
    turn = jnp.arange(most, dtype=jnp.int32)
    chosen = mine[:, None, :] & (rank.astype(jnp.int32)[:, None, :] == turn[None, :, None])
    pick = jnp.sum(jnp.where(chosen, place, 0), axis=-1)

    own_rows = lax.dynamic_index_in_dim(rows, col_id, 0, False)
    own_need = lax.dynamic_index_in_dim(need, col_id, 0, False)
    first = row_id * slots
    own_need = lax.dynamic_slice_in_dim(own_need, first, slots, 0)
    target = lax.dynamic_slice_in_dim(own_rows, first, slots, 0)
    panel = lax.dynamic_index_in_dim(kept_tiles, row_id, 0, False)
    panel_rows = panel[:, 0, :].reshape(-1)
    panel_cols = panel[:, 1, :].reshape(-1)
    same = (panel_rows == target[:, None, None]) & (panel_cols == own_rows[None, :, None])
    spot = jnp.arange(n_col * slots, dtype=jnp.int32)
    spot = nearness(spot // slots, col_id, n_col) * slots + spot % slots
    left = jnp.where(own_need, jnp.sum(jnp.where(same, spot, 0), axis=-1), -1)
    own_chosen = lax.dynamic_index_in_dim(chosen, row_id, 0, False)
    far = jnp.sum(jnp.where(own_chosen[None], left[:, None, :] + 1, 0), axis=-1) - 1
    near = lax.dynamic_slice_in_dim(left, first, slots, 1)
    live = (target >= 0).astype(jnp.int32)
    return largest, pick, jnp.concatenate([near, far], axis=1), live


def local(kept_tiles, density):
    row_id = lax.axis_index("row")
    col_id = lax.axis_index("col")
    n_row, n_col, _, slots = kept_tiles.shape
    tile = density.shape[-1]
    order = n_row * TR * tile
    most = slots * ROW_TILES
    mine = density.reshape(slots, tile, tile)

    def pieces_of(n):
        return jax.ShapeDtypeStruct((n_row, n) + BLOCK, BF16)

    def exchange(x):
        return lax.all_to_all(x, "row", 0, 0, tiled=True)

    def shift(x, axis, inner, size, by):
        n = lax.axis_size(axis)

        def to(i):
            place = i // inner % size
            return i + ((place + by) % size - place) * inner

        return lax.ppermute(x, axis, [(i, to(i)) for i in range(n)])

    def add_over(x, axis, inner, size):
        return sum([shift(x, axis, inner, size, by) for by in range(1, size)], x)

    first = jax.ShapeDtypeStruct((n_row, slots * BLOCK[0] + EXTRA, BLOCK[1]), BF16)
    (pieces,) = kernel_call(prepare_kernel, [(VMEM, first)], [(VMEM, mine)], touched=4 * mine.size)
    held = exchange(pieces)
    largest, pick, left, live = plan(kept_tiles, row_id, col_id, most)
    rows = pick // slots * first.shape[1] + pick % slots * BLOCK[0]
    col_live = lax.dynamic_index_in_dim(kept_tiles, col_id, 1, False)[:, 0, :] >= 0
    lanes = jnp.arange(BLOCK[1], dtype=jnp.int32) // PARTS
    mask = sum(((lanes == s) & col_live[:, s:s + 1]).astype(F32) for s in range(slots))

    def finish(capacity, mine, held, mask, pick, rows, left, live):
        left = left[:, :slots + capacity]
        pick = pick[:, :capacity]
        rows = rows[:, :capacity]
        total = VMEM((slots, tile, tile), F32)
        work = 4 * 2 * tile ** 3
        moved = n_row * capacity * BLOCK[0] * BLOCK[1] * 4
        near = [mine] + [shift(mine, "col", 2, n_col // 2, by) for by in range(1, n_col // 2)]
        panel = jnp.concatenate([x for tiles in near for x in (tiles, shift(tiles, "col", 1, 2, 1))])
        (sent,) = kernel_call(
            select_first_kernel, [(VMEM, pieces_of(capacity))],
            [(SMEM, rows), (VMEM, held.reshape(-1, BLOCK[1]))], touched=moved,
        )
        (sums,) = kernel_call(
            sum_kernel, [(VMEM, jax.ShapeDtypeStruct((8, BLOCK[1]), F32))], [(VMEM, held), (VMEM, mask)]
        )
        sums = add_over(add_over(sums, "col", 2, n_col // 2), "col", 1, 2)
        received = exchange(sent)
        (square,) = kernel_call(
            functools.partial(first_kernel, order), [(VMEM, pieces_of(slots))],
            [(SMEM, left), (SMEM, live), (VMEM, panel), (VMEM, received), (VMEM, mine), (VMEM, sums)],
            scratch=[total],
            flops=work, touched=panel.size,
        )
        (sent,) = kernel_call(
            select_kernel, [(VMEM, pieces_of(capacity))], [(SMEM, pick), (VMEM, exchange(square).reshape((-1,) + BLOCK))], touched=moved,
        )
        received = exchange(sent)
        out = jax.ShapeDtypeStruct((slots, tile, tile), BF16)
        return kernel_call(
            functools.partial(second_kernel, order), [(VMEM, out), (VMEM, out)],
            [(SMEM, left), (SMEM, live), (VMEM, panel), (VMEM, received), (VMEM, square), (VMEM, mine),
             (VMEM, sums)],
            scratch=[total], flops=work, touched=2 * panel.size,
        )

    capacities = sorted({min(c, most) for c in (5, 6, 7, 8, most)})
    branch = sum((largest > c).astype(jnp.int32) for c in capacities[:-1])
    square, updated = lax.switch(
        branch, [functools.partial(finish, c) for c in capacities],
        mine, held, mask, pick, rows, left, live,
    )
    return square.reshape(density.shape), updated.reshape(density.shape)


def solution(mesh):
    spec = P("row", "col", None, None, None)
    return jax.shard_map(local, mesh=mesh, in_specs=(P(), spec), out_specs=(spec, spec), check_vma=False)
```

```python
import functools

import jax
import jax.numpy as jnp
from jax import lax
from jax.experimental import pallas as pl
from jax.experimental.pallas import tpu as pltpu
from jax.sharding import PartitionSpec as P

TR = 4
ROW_TILES = 7
BLOCK = (16, 128)
EXTRA = 8
PARTS = 3
TOGETHER = 4

VMEM = pltpu.VMEM
SMEM = pltpu.SMEM
F32 = jnp.float32
BF16 = jnp.bfloat16


def cut(tile, piece):
    rows, lanes = BLOCK
    half, band = divmod(piece, tile // rows)
    return slice(band * rows, (band + 1) * rows), slice(half * lanes, (half + 1) * lanes)


def whole(ref, q, tile):
    rows, lanes = BLOCK
    bands = tile // rows
    return jnp.concatenate(
        [ref[h * bands:(h + 1) * bands, q].reshape(tile, lanes) for h in range(tile // lanes)], axis=1
    )


def split(value, first, into):
    row = lax.broadcasted_iota(jnp.int32, into.shape, 0)
    lane = lax.broadcasted_iota(jnp.int32, into.shape, 1)
    rest = jnp.full(into.shape, value, F32)
    for t in range(PARTS):
        this = rest.astype(BF16).astype(F32)
        into = jnp.where((row == 0) & (lane == first + t), this, into)
        rest = rest - this
    return into


def prepare_kernel(x_ref, out_ref):
    slots, tile, _ = x_ref.shape
    rows = BLOCK[0]
    sums = jnp.zeros((EXTRA, BLOCK[1]), F32)
    for s in range(slots):
        for p in range(out_ref.shape[0]):
            from_rows, columns = cut(tile, p)
            out_ref[p, s * rows:(s + 1) * rows] = x_ref[s, from_rows, columns]
        value = x_ref[s].astype(F32)
        part = jnp.sum((value * value).reshape(tile // 8, 8, tile), axis=0)
        sums = split(jnp.sum(part), s * PARTS, sums)
    for p in range(out_ref.shape[0]):
        out_ref[p, slots * rows:] = sums.astype(BF16)


def select(turn, pick_ref, fetch, out_ref):
    n_to, capacity = out_ref.shape[:2]

    def body(n, _):
        spots = [(n * TOGETHER + d, q) for d in range(TOGETHER) for q in range(capacity)]
        values = [fetch(pick_ref[turn, d, q]) for d, q in spots]
        for (d, q), value in zip(spots, values):
            out_ref[d, q] = value
        return 0

    lax.fori_loop(0, n_to // TOGETHER, body, 0)


def select_kernel(pick_ref, held_ref, out_ref):
    select(1, pick_ref, lambda place: held_ref[place], out_ref)


def select_first_kernel(pick_ref, held_ref, out_ref):
    rows = BLOCK[0]
    select(0, pick_ref, lambda row: held_ref[pl.ds(pl.multiple_of(row, 8), rows)], out_ref)


def sum_kernel(held_ref, mask_ref, out_ref):
    parts = held_ref[:, held_ref.shape[1] - EXTRA:].astype(F32)
    out_ref[...] = jnp.full(out_ref.shape, jnp.sum(jnp.sum(parts, axis=1) * mask_ref[...]), F32)


def accumulate(left_ref, left_tile, received_ref, own, total_ref, targets, turns_ref):
    slots, tile, _ = total_ref.shape
    capacity = received_ref.shape[1]

    for u in targets:
        total_ref[u] = jnp.zeros((tile, tile), F32)
        for v in range(slots):
            @pl.when(left_ref[u, v] >= 0)
            def _():
                total_ref[u] += jnp.dot(left_tile(u, v), own(v), preferred_element_type=F32)

        count = jnp.int32(0)
        for q in range(capacity):
            turns_ref[count] = q
            count += (left_ref[u, slots + q] >= 0).astype(jnp.int32)

        def body(n, _, u=u):
            q = turns_ref[2 * n]
            again = turns_ref[2 * n + 1]
            total_ref[u] += jnp.dot(
                jnp.concatenate([left_tile(u, slots + q), left_tile(u, slots + again)], axis=1),
                jnp.concatenate([whole(received_ref, q, tile), whole(received_ref, again, tile)], axis=0),
                preferred_element_type=F32,
            )
            return 0

        lax.fori_loop(0, count // 2, body, 0)

        @pl.when(count % 2 > 0)
        def _(u=u, count=count):
            q = turns_ref[count - 1]
            total_ref[u] += jnp.dot(left_tile(u, slots + q), whole(received_ref, q, tile), preferred_element_type=F32)


def scale_of(sums_ref, order):
    return (2.0 * jnp.sqrt(sums_ref[0:1] / order))[:, 0:1]


def left_from(panel_ref, left_ref):
    def left_tile(u, n):
        return panel_ref[jnp.maximum(left_ref[u, n], 0)]

    return left_tile


def first_kernel(order, left_ref, live_ref, panel_ref, received_ref, x_ref, sums_ref, pieces_ref,
                 total_ref, turns_ref, left_tiles, sems):
    slots, tile, _ = total_ref.shape
    turns = left_ref.shape[1]

    def fetch(u, n):
        spot = u * turns + n
        return pltpu.make_async_copy(panel_ref.at[jnp.maximum(left_ref[u, n], 0)], left_tiles.at[spot], sems.at[spot])

    for u in range(slots):
        for n in range(turns):
            @pl.when(left_ref[u, n] >= 0)
            def _():
                fetch(u, n).start()

    def left_tile(u, n):
        fetch(u, n).wait()
        return left_tiles[u * turns + n]

    scale = scale_of(sums_ref, order)
    accumulate(left_ref, left_tile, received_ref, lambda v: x_ref[v], total_ref, range(slots), turns_ref)
    for s in range(slots):
        square = jnp.where(live_ref[s] > 0, total_ref[s] / scale, 0.0).astype(BF16)
        for p in range(pieces_ref.shape[0]):
            rows, columns = cut(tile, p)
            pieces_ref[p, s] = square[rows, columns]


def second_kernel(order, left_ref, live_ref, panel_ref, received_ref, own_ref, x_ref, sums_ref,
                  square_ref, updated_ref, total_ref, turns_ref, square, updated, sems):
    slots, tile, _ = total_ref.shape
    moves = []

    def send(s, value, to_ref):
        move = pltpu.make_async_copy(value.at[s], to_ref.at[s], sems.at[len(moves)])
        move.start()
        moves.append(move)

    for s in range(slots):
        square[s] = whole(own_ref, s, tile)
        send(s, square, square_ref)
    scale = scale_of(sums_ref, order)
    for u in range(slots):
        accumulate(left_ref, left_from(panel_ref, left_ref), received_ref, lambda v: square[v], total_ref,
                   [u], turns_ref)
        new = 1.5 * x_ref[u].astype(F32) - 0.5 * total_ref[u] / scale
        updated[u] = jnp.where(live_ref[u] > 0, new, 0.0).astype(BF16)
        send(u, updated, updated_ref)
    for move in moves:
        move.wait()


def kernel_call(body, outs, ins, scratch=(), flops=0, touched=0):
    return pl.pallas_call(
        body,
        out_shape=[shape for _, shape in outs],
        in_specs=[pl.BlockSpec(memory_space=space) for space, _ in ins],
        out_specs=[pl.BlockSpec(memory_space=space) for space, _ in outs],
        scratch_shapes=list(scratch),
        compiler_params=pltpu.CompilerParams(vmem_limit_bytes=40 * 1024 * 1024),
        cost_estimate=pl.CostEstimate(flops=flops, bytes_accessed=touched, transcendentals=0),
    )(*[value for _, value in ins])


def plan(kept_tiles, row_id, col_id, most):
    n_row, n_col, _, slots = kept_tiles.shape
    size = n_row * TR
    held = n_row * slots
    rows = kept_tiles[:, :, 0, :].transpose(1, 0, 2).reshape(n_col, held)
    cols = kept_tiles[:, :, 1, :].transpose(1, 0, 2).reshape(n_col, held)
    ids = jnp.arange(size, dtype=jnp.int32)
    hot_rows = (rows[:, :, None] == ids).astype(jnp.bfloat16)
    hot_cols = (cols[:, :, None] == ids).astype(jnp.bfloat16)
    pattern = jnp.einsum("gsi,gsk->ik", hot_rows, hot_cols).astype(jnp.bfloat16)
    reach = jnp.einsum("gti,ik->gtk", hot_rows, pattern).astype(jnp.bfloat16)
    meet = jnp.einsum("gtk,gsk->gts", reach, hot_rows)
    need = (meet > 0) & (cols[:, :, None] == cols[:, None, :])
    place = jnp.arange(held, dtype=jnp.int32)
    devices = jnp.arange(n_row, dtype=jnp.int32)
    remote = devices[:, None] != place[None, :] // slots
    wanted = need.reshape(n_col, n_row, slots, held).any(2) & remote
    largest = jnp.max(jnp.sum(wanted.astype(jnp.int32), axis=-1))

    mine = lax.dynamic_index_in_dim(wanted, col_id, 0, False)
    before = (place[:, None] < place[None, :]).astype(jnp.bfloat16)
    rank = jnp.dot(mine.astype(jnp.bfloat16), before, preferred_element_type=jnp.float32)
    turn = jnp.arange(most, dtype=jnp.int32)
    chosen = mine[:, None, :] & (rank.astype(jnp.int32)[:, None, :] == turn[None, :, None])
    pick = jnp.sum(jnp.where(chosen, place, 0), axis=-1)

    own_rows = lax.dynamic_index_in_dim(rows, col_id, 0, False)
    own_need = lax.dynamic_index_in_dim(need, col_id, 0, False)
    first = row_id * slots
    own_need = lax.dynamic_slice_in_dim(own_need, first, slots, 0)
    target = lax.dynamic_slice_in_dim(own_rows, first, slots, 0)
    panel = lax.dynamic_index_in_dim(kept_tiles, row_id, 0, False)
    panel_rows = panel[:, 0, :].reshape(-1)
    panel_cols = panel[:, 1, :].reshape(-1)
    same = (panel_rows == target[:, None, None]) & (panel_cols == own_rows[None, :, None])
    spot = jnp.arange(n_col * slots, dtype=jnp.int32)
    left = jnp.where(own_need, jnp.sum(jnp.where(same, spot, 0), axis=-1), -1)
    own_chosen = lax.dynamic_index_in_dim(chosen, row_id, 0, False)
    far = jnp.sum(jnp.where(own_chosen[None], left[:, None, :] + 1, 0), axis=-1) - 1
    near = lax.dynamic_slice_in_dim(left, first, slots, 1)
    live = (target >= 0).astype(jnp.int32)
    return largest, pick, jnp.concatenate([near, far], axis=1), live


def local(kept_tiles, density):
    row_id = lax.axis_index("row")
    col_id = lax.axis_index("col")
    n_row, n_col, _, slots = kept_tiles.shape
    tile = density.shape[-1]
    order = n_row * TR * tile
    most = slots * ROW_TILES
    mine = density.reshape(slots, tile, tile)

    def pieces_of(n):
        return jax.ShapeDtypeStruct((n_row, n) + BLOCK, BF16)

    def exchange(x):
        return lax.all_to_all(x, "row", 0, 0, tiled=True)

    def add_over(total, axis, inner, size):
        n = lax.axis_size(axis)

        def moved(i, by):
            place = i // inner % size
            return i + ((place + by) % size - place) * inner

        parts = [lax.ppermute(total, axis, [(i, moved(i, by)) for i in range(n)]) for by in range(1, size)]
        return sum(parts, total)

    first = jax.ShapeDtypeStruct((n_row, slots * BLOCK[0] + EXTRA, BLOCK[1]), BF16)
    (pieces,) = kernel_call(prepare_kernel, [(VMEM, first)], [(VMEM, mine)], touched=4 * mine.size)
    held = exchange(pieces)
    largest, pick, left, live = plan(kept_tiles, row_id, col_id, most)
    pick = jnp.stack([pick // slots * first.shape[1] + pick % slots * BLOCK[0], pick])
    col_live = lax.dynamic_index_in_dim(kept_tiles, col_id, 1, False)[:, 0, :] >= 0
    lanes = jnp.arange(BLOCK[1], dtype=jnp.int32) // PARTS
    mask = sum(((lanes == s) & col_live[:, s:s + 1]).astype(F32) for s in range(slots))

    def finish(capacity, mine, held, mask, pick, left, live):
        left = left[:, :slots + capacity]
        total = VMEM((slots, tile, tile), F32)
        turns = SMEM((capacity + 1,), jnp.int32)
        work = 4 * 2 * tile ** 3
        moved = n_row * capacity * BLOCK[0] * BLOCK[1] * 4
        panel = lax.all_gather(mine, "col", axis=0, tiled=True)
        (sent,) = kernel_call(
            select_first_kernel, [(VMEM, pieces_of(capacity))],
            [(SMEM, pick), (VMEM, held.reshape(-1, BLOCK[1]))], touched=moved,
        )
        (sums,) = kernel_call(
            sum_kernel, [(VMEM, jax.ShapeDtypeStruct((8, BLOCK[1]), F32))], [(VMEM, held), (VMEM, mask)]
        )
        sums = add_over(add_over(sums, "col", 2, n_col // 2), "col", 1, 2)
        received = exchange(sent)
        (square,) = kernel_call(
            functools.partial(first_kernel, order), [(VMEM, pieces_of(slots))],
            [(SMEM, left), (SMEM, live), (pltpu.HBM, pltpu.with_memory_space_constraint(panel, pltpu.HBM)), (VMEM, received),
             (VMEM, mine), (VMEM, sums)],
            scratch=[
                total, turns, VMEM((slots * left.shape[1], tile, tile), BF16),
                pltpu.SemaphoreType.DMA((slots * left.shape[1],)),
            ],
            flops=work, touched=panel.size,
        )
        (sent,) = kernel_call(
            select_kernel, [(VMEM, pieces_of(capacity))], [(SMEM, pick), (VMEM, exchange(square).reshape((-1,) + BLOCK))], touched=moved,
        )
        received = exchange(sent)
        out = jax.ShapeDtypeStruct((slots, tile, tile), BF16)
        return kernel_call(
            functools.partial(second_kernel, order), [(pl.ANY, out), (pl.ANY, out)],
            [(SMEM, left), (SMEM, live), (VMEM, panel), (VMEM, received), (VMEM, square), (VMEM, mine),
             (VMEM, sums)],
            scratch=[total, turns, VMEM(out.shape, BF16), VMEM(out.shape, BF16), pltpu.SemaphoreType.DMA((2 * slots,))],
            flops=work, touched=2 * panel.size,
        )

    capacities = sorted({min(c, most) for c in (5, 6, 7, 8, most)})
    branch = sum((largest > c).astype(jnp.int32) for c in capacities[:-1])
    square, updated = lax.switch(
        branch, [functools.partial(finish, c) for c in capacities],
        mine, held, mask, pick, left, live,
    )
    return square.reshape(density.shape), updated.reshape(density.shape)


def solution(mesh):
    spec = P("row", "col", None, None, None)
    return jax.shard_map(local, mesh=mesh, in_specs=(P(), spec), out_specs=(spec, spec), check_vma=False)
```

```python
import functools

import jax
import jax.numpy as jnp
from jax import lax
from jax.experimental import pallas as pl
from jax.experimental.pallas import tpu as pltpu
from jax.sharding import PartitionSpec as P

TR = 4
ROW_TILES = 7
BLOCK = (16, 128)
EXTRA = 8
PARTS = 3
TOGETHER = 4

VMEM = pltpu.VMEM
SMEM = pltpu.SMEM
F32 = jnp.float32
BF16 = jnp.bfloat16


def cut(tile, piece):
    rows, lanes = BLOCK
    half, band = divmod(piece, tile // rows)
    return slice(band * rows, (band + 1) * rows), slice(half * lanes, (half + 1) * lanes)


def whole(ref, q, tile):
    rows, lanes = BLOCK
    bands = tile // rows
    return jnp.concatenate(
        [ref[h * bands:(h + 1) * bands, q].reshape(tile, lanes) for h in range(tile // lanes)], axis=1
    )


def split(value, first, into):
    row = lax.broadcasted_iota(jnp.int32, into.shape, 0)
    lane = lax.broadcasted_iota(jnp.int32, into.shape, 1)
    rest = jnp.full(into.shape, value, F32)
    for t in range(PARTS):
        this = rest.astype(BF16).astype(F32)
        into = jnp.where((row == 0) & (lane == first + t), this, into)
        rest = rest - this
    return into


def prepare_kernel(x_ref, out_ref):
    slots, tile, _ = x_ref.shape
    rows = BLOCK[0]
    sums = jnp.zeros((EXTRA, BLOCK[1]), F32)
    for s in range(slots):
        for p in range(out_ref.shape[0]):
            from_rows, columns = cut(tile, p)
            out_ref[p, s * rows:(s + 1) * rows] = x_ref[s, from_rows, columns]
        value = x_ref[s].astype(F32)
        part = jnp.sum((value * value).reshape(tile // 8, 8, tile), axis=0)
        sums = split(jnp.sum(part), s * PARTS, sums)
    for p in range(out_ref.shape[0]):
        out_ref[p, slots * rows:] = sums.astype(BF16)


def select(turn, pick_ref, fetch, out_ref):
    n_to, capacity = out_ref.shape[:2]

    def body(n, _):
        spots = [(n * TOGETHER + d, q) for d in range(TOGETHER) for q in range(capacity)]
        values = [fetch(pick_ref[turn, d, q]) for d, q in spots]
        for (d, q), value in zip(spots, values):
            out_ref[d, q] = value
        return 0

    lax.fori_loop(0, n_to // TOGETHER, body, 0)


def select_kernel(pick_ref, held_ref, out_ref):
    select(1, pick_ref, lambda place: held_ref[place], out_ref)


def select_sum_kernel(pick_ref, held_ref, flat_ref, x_ref, mask_ref, share_ref, out_ref, tail, sems):
    slots, tile, _ = x_ref.shape
    rows = BLOCK[0]
    moves = [
        pltpu.make_async_copy(x_ref.at[s], share_ref.at[pl.ds(s * tile, tile)], sems.at[s]) for s in range(slots)
    ] + [pltpu.make_async_copy(tail, share_ref.at[pl.ds(slots * tile, rows)], sems.at[slots])]
    for move in moves[:slots]:
        move.start()
    parts = held_ref[:, held_ref.shape[1] - EXTRA:].astype(F32)
    total = jnp.sum(jnp.sum(parts, axis=1) * mask_ref[...])
    tail[...] = split(total, 0, jnp.zeros(tail.shape, F32)).astype(BF16)
    moves[slots].start()
    select(0, pick_ref, lambda row: flat_ref[pl.ds(pl.multiple_of(row, 8), rows)], out_ref)
    for move in moves:
        move.wait()


def accumulate(left_ref, left_tile, received_ref, own, total_ref, targets, turns_ref):
    slots, tile, _ = total_ref.shape
    capacity = received_ref.shape[1]

    for u in targets:
        total_ref[u] = jnp.zeros((tile, tile), F32)
        for v in range(slots):
            @pl.when(left_ref[u, v] >= 0)
            def _():
                total_ref[u] += jnp.dot(left_tile(u, v), own(v), preferred_element_type=F32)

        count = jnp.int32(0)
        for q in range(capacity):
            turns_ref[count] = q
            count += (left_ref[u, slots + q] >= 0).astype(jnp.int32)

        def body(n, _, u=u):
            q = turns_ref[2 * n]
            again = turns_ref[2 * n + 1]
            total_ref[u] += jnp.dot(
                jnp.concatenate([left_tile(u, slots + q), left_tile(u, slots + again)], axis=1),
                jnp.concatenate([whole(received_ref, q, tile), whole(received_ref, again, tile)], axis=0),
                preferred_element_type=F32,
            )
            return 0

        lax.fori_loop(0, count // 2, body, 0)

        @pl.when(count % 2 > 0)
        def _(u=u, count=count):
            q = turns_ref[count - 1]
            total_ref[u] += jnp.dot(left_tile(u, slots + q), whole(received_ref, q, tile), preferred_element_type=F32)


def scale_of(sums_ref, order):
    return (2.0 * jnp.sqrt(sums_ref[0:1] / order))[:, 0:1]


def left_from(panel_ref, left_ref):
    def left_tile(u, n):
        return panel_ref[pl.ds(pl.multiple_of(jnp.maximum(left_ref[u, n], 0), 16), panel_ref.shape[1])]

    return left_tile


def first_kernel(order, left_ref, live_ref, panel_ref, received_ref, x_ref, pieces_ref, sums_ref,
                 total_ref, turns_ref, left_tiles, tails, sems, tail_sems):
    slots, tile, _ = total_ref.shape
    turns = left_ref.shape[1]
    share = panel_ref.shape[0] // tails.shape[0]
    ends = [
        pltpu.make_async_copy(
            panel_ref.at[pl.ds(c * share + slots * tile, BLOCK[0]), pl.ds(0, BLOCK[1])], tails.at[c], tail_sems.at[c])
        for c in range(tails.shape[0])
    ]

    def fetch(u, n):
        spot = u * turns + n
        row = pl.multiple_of(jnp.maximum(left_ref[u, n], 0), 16)
        return pltpu.make_async_copy(panel_ref.at[pl.ds(row, tile)], left_tiles.at[spot], sems.at[spot])

    for u in range(slots):
        for n in range(turns):
            @pl.when(left_ref[u, n] >= 0)
            def _():
                fetch(u, n).start()
    for end in ends:
        end.start()

    def left_tile(u, n):
        fetch(u, n).wait()
        return left_tiles[u * turns + n]

    accumulate(left_ref, left_tile, received_ref, lambda v: x_ref[v], total_ref, range(slots), turns_ref)
    for end in ends:
        end.wait()
    sums_ref[...] = jnp.full(sums_ref.shape, jnp.sum(jnp.sum(tails[...].astype(F32), axis=0)), F32)
    scale = scale_of(sums_ref, order)
    for s in range(slots):
        square = jnp.where(live_ref[s] > 0, total_ref[s] / scale, 0.0).astype(BF16)
        for p in range(pieces_ref.shape[0]):
            rows, columns = cut(tile, p)
            pieces_ref[p, s] = square[rows, columns]


def second_kernel(order, left_ref, live_ref, panel_ref, received_ref, own_ref, x_ref, sums_ref,
                  square_ref, updated_ref, total_ref, turns_ref, square, updated, sems):
    slots, tile, _ = total_ref.shape
    moves = []

    def send(s, value, to_ref):
        move = pltpu.make_async_copy(value.at[s], to_ref.at[s], sems.at[len(moves)])
        move.start()
        moves.append(move)

    for s in range(slots):
        square[s] = whole(own_ref, s, tile)
        send(s, square, square_ref)
    scale = scale_of(sums_ref, order)
    for u in range(slots):
        accumulate(left_ref, left_from(panel_ref, left_ref), received_ref, lambda v: square[v], total_ref,
                   [u], turns_ref)
        new = 1.5 * x_ref[u].astype(F32) - 0.5 * total_ref[u] / scale
        updated[u] = jnp.where(live_ref[u] > 0, new, 0.0).astype(BF16)
        send(u, updated, updated_ref)
    for move in moves:
        move.wait()


def kernel_call(body, outs, ins, scratch=(), flops=0, touched=0):
    return pl.pallas_call(
        body,
        out_shape=[shape for _, shape in outs],
        in_specs=[pl.BlockSpec(memory_space=space) for space, _ in ins],
        out_specs=[pl.BlockSpec(memory_space=space) for space, _ in outs],
        scratch_shapes=list(scratch),
        compiler_params=pltpu.CompilerParams(vmem_limit_bytes=40 * 1024 * 1024),
        cost_estimate=pl.CostEstimate(flops=flops, bytes_accessed=touched, transcendentals=0),
    )(*[value for _, value in ins])


def plan(kept_tiles, row_id, col_id, most, tile):
    n_row, n_col, _, slots = kept_tiles.shape
    size = n_row * TR
    held = n_row * slots
    rows = kept_tiles[:, :, 0, :].transpose(1, 0, 2).reshape(n_col, held)
    cols = kept_tiles[:, :, 1, :].transpose(1, 0, 2).reshape(n_col, held)
    ids = jnp.arange(size, dtype=jnp.int32)
    hot_rows = (rows[:, :, None] == ids).astype(jnp.bfloat16)
    hot_cols = (cols[:, :, None] == ids).astype(jnp.bfloat16)
    pattern = jnp.einsum("gsi,gsk->ik", hot_rows, hot_cols).astype(jnp.bfloat16)
    reach = jnp.einsum("gti,ik->gtk", hot_rows, pattern).astype(jnp.bfloat16)
    meet = jnp.einsum("gtk,gsk->gts", reach, hot_rows)
    need = (meet > 0) & (cols[:, :, None] == cols[:, None, :])
    place = jnp.arange(held, dtype=jnp.int32)
    devices = jnp.arange(n_row, dtype=jnp.int32)
    remote = devices[:, None] != place[None, :] // slots
    wanted = need.reshape(n_col, n_row, slots, held).any(2) & remote
    largest = jnp.max(jnp.sum(wanted.astype(jnp.int32), axis=-1))

    mine = lax.dynamic_index_in_dim(wanted, col_id, 0, False)
    before = (place[:, None] < place[None, :]).astype(jnp.bfloat16)
    rank = jnp.dot(mine.astype(jnp.bfloat16), before, preferred_element_type=jnp.float32)
    turn = jnp.arange(most, dtype=jnp.int32)
    chosen = mine[:, None, :] & (rank.astype(jnp.int32)[:, None, :] == turn[None, :, None])
    pick = jnp.sum(jnp.where(chosen, place, 0), axis=-1)

    own_rows = lax.dynamic_index_in_dim(rows, col_id, 0, False)
    own_need = lax.dynamic_index_in_dim(need, col_id, 0, False)
    first = row_id * slots
    own_need = lax.dynamic_slice_in_dim(own_need, first, slots, 0)
    target = lax.dynamic_slice_in_dim(own_rows, first, slots, 0)
    panel = lax.dynamic_index_in_dim(kept_tiles, row_id, 0, False)
    panel_rows = panel[:, 0, :].reshape(-1)
    panel_cols = panel[:, 1, :].reshape(-1)
    same = (panel_rows == target[:, None, None]) & (panel_cols == own_rows[None, :, None])
    spot = jnp.arange(n_col * slots, dtype=jnp.int32)
    spot = spot // slots * (slots * tile + BLOCK[0]) + spot % slots * tile
    left = jnp.where(own_need, jnp.sum(jnp.where(same, spot, 0), axis=-1), -1)
    own_chosen = lax.dynamic_index_in_dim(chosen, row_id, 0, False)
    far = jnp.sum(jnp.where(own_chosen[None], left[:, None, :] + 1, 0), axis=-1) - 1
    near = lax.dynamic_slice_in_dim(left, first, slots, 1)
    live = (target >= 0).astype(jnp.int32)
    return largest, pick, jnp.concatenate([near, far], axis=1), live


def local(kept_tiles, density):
    row_id = lax.axis_index("row")
    col_id = lax.axis_index("col")
    n_row, n_col, _, slots = kept_tiles.shape
    tile = density.shape[-1]
    order = n_row * TR * tile
    most = slots * ROW_TILES
    mine = density.reshape(slots, tile, tile)

    def pieces_of(n):
        return jax.ShapeDtypeStruct((n_row, n) + BLOCK, BF16)

    def exchange(x):
        return lax.all_to_all(x, "row", 0, 0, tiled=True)

    first = jax.ShapeDtypeStruct((n_row, slots * BLOCK[0] + EXTRA, BLOCK[1]), BF16)
    (pieces,) = kernel_call(prepare_kernel, [(VMEM, first)], [(VMEM, mine)], touched=4 * mine.size)
    held = exchange(pieces)
    largest, pick, left, live = plan(kept_tiles, row_id, col_id, most, tile)
    pick = jnp.stack([pick // slots * first.shape[1] + pick % slots * BLOCK[0], pick])
    col_live = lax.dynamic_index_in_dim(kept_tiles, col_id, 1, False)[:, 0, :] >= 0
    lanes = jnp.arange(BLOCK[1], dtype=jnp.int32) // PARTS
    mask = sum(((lanes == s) & col_live[:, s:s + 1]).astype(F32) for s in range(slots))

    def finish(capacity, mine, held, mask, pick, left, live):
        left = left[:, :slots + capacity]
        total = VMEM((slots, tile, tile), F32)
        turns = SMEM((capacity + 1,), jnp.int32)
        work = 4 * 2 * tile ** 3
        moved = n_row * capacity * BLOCK[0] * BLOCK[1] * 4
        share, sent = kernel_call(
            select_sum_kernel,
            [(pl.ANY, jax.ShapeDtypeStruct((slots * tile + BLOCK[0], tile), BF16)), (VMEM, pieces_of(capacity))],
            [(SMEM, pick), (VMEM, held), (VMEM, held.reshape(-1, BLOCK[1])), (pl.ANY, mine), (VMEM, mask)],
            scratch=[VMEM((BLOCK[0], tile), BF16), pltpu.SemaphoreType.DMA((slots + 1,))], touched=moved,
        )
        panel = lax.all_gather(share, "col", axis=0, tiled=True)
        received = exchange(sent)
        square, sums = kernel_call(
            functools.partial(first_kernel, order),
            [(VMEM, pieces_of(slots)), (VMEM, jax.ShapeDtypeStruct((8, BLOCK[1]), F32))],
            [(SMEM, left), (SMEM, live), (pltpu.HBM, pltpu.with_memory_space_constraint(panel, pltpu.HBM)), (VMEM, received),
             (VMEM, mine)],
            scratch=[
                total, turns, VMEM((slots * left.shape[1], tile, tile), BF16),
                VMEM((n_col,) + BLOCK, BF16),
                pltpu.SemaphoreType.DMA((slots * left.shape[1],)), pltpu.SemaphoreType.DMA((n_col,)),
            ],
            flops=work, touched=panel.size,
        )
        (sent,) = kernel_call(
            select_kernel, [(VMEM, pieces_of(capacity))], [(SMEM, pick), (VMEM, exchange(square).reshape((-1,) + BLOCK))], touched=moved,
        )
        received = exchange(sent)
        out = jax.ShapeDtypeStruct((slots, tile, tile), BF16)
        return kernel_call(
            functools.partial(second_kernel, order), [(pl.ANY, out), (pl.ANY, out)],
            [(SMEM, left), (SMEM, live), (VMEM, panel), (VMEM, received), (VMEM, square), (VMEM, mine),
             (VMEM, sums)],
            scratch=[total, turns, VMEM(out.shape, BF16), VMEM(out.shape, BF16), pltpu.SemaphoreType.DMA((2 * slots,))],
            flops=work, touched=2 * panel.size,
        )

    capacities = sorted({min(c, most) for c in (5, 6, 7, 8, most)})
    branch = sum((largest > c).astype(jnp.int32) for c in capacities[:-1])
    square, updated = lax.switch(
        branch, [functools.partial(finish, c) for c in capacities],
        mine, held, mask, pick, left, live,
    )
    return square.reshape(density.shape), updated.reshape(density.shape)


def solution(mesh):
    spec = P("row", "col", None, None, None)
    return jax.shard_map(local, mesh=mesh, in_specs=(P(), spec), out_specs=(spec, spec), check_vma=False)
```

```python
import functools

import jax
import jax.numpy as jnp
from jax import lax
from jax.experimental import pallas as pl
from jax.experimental.pallas import tpu as pltpu
from jax.sharding import PartitionSpec as P

TR = 4
ROW_TILES = 7
BLOCK = (16, 128)
EXTRA = 8
PARTS = 3
TOGETHER = 4

VMEM = pltpu.VMEM
SMEM = pltpu.SMEM
F32 = jnp.float32
BF16 = jnp.bfloat16


def cut(tile, piece):
    rows, lanes = BLOCK
    half, band = divmod(piece, tile // rows)
    return slice(band * rows, (band + 1) * rows), slice(half * lanes, (half + 1) * lanes)


def whole(ref, q, tile):
    rows, lanes = BLOCK
    bands = tile // rows
    return jnp.concatenate(
        [ref[h * bands:(h + 1) * bands, q].reshape(tile, lanes) for h in range(tile // lanes)], axis=1
    )


def split(value, first, into):
    row = lax.broadcasted_iota(jnp.int32, into.shape, 0)
    lane = lax.broadcasted_iota(jnp.int32, into.shape, 1)
    rest = jnp.full(into.shape, value, F32)
    for t in range(PARTS):
        this = rest.astype(BF16).astype(F32)
        into = jnp.where((row == 0) & (lane == first + t), this, into)
        rest = rest - this
    return into


def prepare_kernel(x_ref, out_ref):
    slots, tile, _ = x_ref.shape
    rows = BLOCK[0]
    sums = jnp.zeros((EXTRA, BLOCK[1]), F32)
    for s in range(slots):
        for p in range(out_ref.shape[0]):
            from_rows, columns = cut(tile, p)
            out_ref[p, s * rows:(s + 1) * rows] = x_ref[s, from_rows, columns]
        value = x_ref[s].astype(F32)
        part = jnp.sum((value * value).reshape(tile // 8, 8, tile), axis=0)
        sums = split(jnp.sum(part), s * PARTS, sums)
    for p in range(out_ref.shape[0]):
        out_ref[p, slots * rows:] = sums.astype(BF16)


def select(turn, pick_ref, fetch, out_ref):
    n_to, capacity = out_ref.shape[:2]

    def body(n, _):
        spots = [(n * TOGETHER + d, q) for d in range(TOGETHER) for q in range(capacity)]
        values = [fetch(pick_ref[turn, d, q]) for d, q in spots]
        for (d, q), value in zip(spots, values):
            out_ref[d, q] = value
        return 0

    lax.fori_loop(0, n_to // TOGETHER, body, 0)


def select_kernel(pick_ref, held_ref, out_ref):
    select(1, pick_ref, lambda place: held_ref[place], out_ref)


def select_first_kernel(pick_ref, held_ref, out_ref):
    rows = BLOCK[0]
    select(0, pick_ref, lambda row: held_ref[pl.ds(pl.multiple_of(row, 8), rows)], out_ref)


def sum_kernel(held_ref, mask_ref, out_ref):
    parts = held_ref[:, held_ref.shape[1] - EXTRA:].astype(F32)
    out_ref[...] = jnp.full(out_ref.shape, jnp.sum(jnp.sum(parts, axis=1) * mask_ref[...]), F32)


def accumulate(left_ref, left_tile, received_ref, own, total_ref, targets, turns_ref):
    slots, tile, _ = total_ref.shape
    capacity = received_ref.shape[1]

    for u in targets:
        total_ref[u] = jnp.zeros((tile, tile), F32)
        for v in range(slots):
            @pl.when(left_ref[u, v] >= 0)
            def _():
                total_ref[u] += jnp.dot(left_tile(u, v), own(v), preferred_element_type=F32)

        count = jnp.int32(0)
        for q in range(capacity):
            turns_ref[count] = q
            count += (left_ref[u, slots + q] >= 0).astype(jnp.int32)

        def body(n, _, u=u):
            q = turns_ref[2 * n]
            again = turns_ref[2 * n + 1]
            total_ref[u] += jnp.dot(
                jnp.concatenate([left_tile(u, slots + q), left_tile(u, slots + again)], axis=1),
                jnp.concatenate([whole(received_ref, q, tile), whole(received_ref, again, tile)], axis=0),
                preferred_element_type=F32,
            )
            return 0

        lax.fori_loop(0, count // 2, body, 0)

        @pl.when(count % 2 > 0)
        def _(u=u, count=count):
            q = turns_ref[count - 1]
            total_ref[u] += jnp.dot(left_tile(u, slots + q), whole(received_ref, q, tile), preferred_element_type=F32)


def inverse_scale(sums_ref, order):
    return (1.0 / (2.0 * jnp.sqrt(sums_ref[0:1] / order)))[:, 0:1]


def left_from(panel_ref, left_ref):
    def left_tile(u, n):
        return panel_ref[jnp.maximum(left_ref[u, n], 0)]

    return left_tile


def first_kernel(order, left_ref, live_ref, panel_ref, received_ref, x_ref, sums_ref, pieces_ref,
                 total_ref, turns_ref, left_tiles, sems):
    slots, tile, _ = total_ref.shape
    turns = left_ref.shape[1]

    def fetch(u, n):
        spot = u * turns + n
        return pltpu.make_async_copy(panel_ref.at[jnp.maximum(left_ref[u, n], 0)], left_tiles.at[spot], sems.at[spot])

    for u in range(slots):
        for n in range(turns):
            @pl.when(left_ref[u, n] >= 0)
            def _():
                fetch(u, n).start()

    def left_tile(u, n):
        fetch(u, n).wait()
        return left_tiles[u * turns + n]

    inverse = inverse_scale(sums_ref, order)
    accumulate(left_ref, left_tile, received_ref, lambda v: x_ref[v], total_ref, range(slots), turns_ref)
    for s in range(slots):
        square = jnp.where(live_ref[s] > 0, total_ref[s] * inverse, 0.0).astype(BF16)
        for p in range(pieces_ref.shape[0]):
            rows, columns = cut(tile, p)
            pieces_ref[p, s] = square[rows, columns]


def second_kernel(order, left_ref, live_ref, panel_ref, received_ref, own_ref, x_ref, sums_ref,
                  square_ref, updated_ref, total_ref, turns_ref, square, updated, sems):
    slots, tile, _ = total_ref.shape
    moves = []

    def send(s, value, to_ref):
        move = pltpu.make_async_copy(value.at[s], to_ref.at[s], sems.at[len(moves)])
        move.start()
        moves.append(move)

    for s in range(slots):
        square[s] = whole(own_ref, s, tile)
        send(s, square, square_ref)
    inverse = inverse_scale(sums_ref, order)
    for u in range(slots):
        accumulate(left_ref, left_from(panel_ref, left_ref), received_ref, lambda v: square[v], total_ref,
                   [u], turns_ref)
        new = 1.5 * x_ref[u].astype(F32) - (0.5 * inverse) * total_ref[u]
        updated[u] = jnp.where(live_ref[u] > 0, new, 0.0).astype(BF16)
        send(u, updated, updated_ref)
    for move in moves:
        move.wait()


def kernel_call(body, outs, ins, scratch=(), flops=0, touched=0):
    return pl.pallas_call(
        body,
        out_shape=[shape for _, shape in outs],
        in_specs=[pl.BlockSpec(memory_space=space) for space, _ in ins],
        out_specs=[pl.BlockSpec(memory_space=space) for space, _ in outs],
        scratch_shapes=list(scratch),
        compiler_params=pltpu.CompilerParams(vmem_limit_bytes=40 * 1024 * 1024),
        cost_estimate=pl.CostEstimate(flops=flops, bytes_accessed=touched, transcendentals=0),
    )(*[value for _, value in ins])


def plan(kept_tiles, row_id, col_id, most):
    n_row, n_col, _, slots = kept_tiles.shape
    size = n_row * TR
    held = n_row * slots
    rows = kept_tiles[:, :, 0, :].transpose(1, 0, 2).reshape(n_col, held)
    cols = kept_tiles[:, :, 1, :].transpose(1, 0, 2).reshape(n_col, held)
    ids = jnp.arange(size, dtype=jnp.int32)
    hot_rows = (rows[:, :, None] == ids).astype(jnp.bfloat16)
    hot_cols = (cols[:, :, None] == ids).astype(jnp.bfloat16)
    pattern = jnp.einsum("gsi,gsk->ik", hot_rows, hot_cols).astype(jnp.bfloat16)
    reach = jnp.einsum("gti,ik->gtk", hot_rows, pattern).astype(jnp.bfloat16)
    meet = jnp.einsum("gtk,gsk->gts", reach, hot_rows)
    need = (meet > 0) & (cols[:, :, None] == cols[:, None, :])
    place = jnp.arange(held, dtype=jnp.int32)
    devices = jnp.arange(n_row, dtype=jnp.int32)
    remote = devices[:, None] != place[None, :] // slots
    wanted = need.reshape(n_col, n_row, slots, held).any(2) & remote
    largest = jnp.max(jnp.sum(wanted.astype(jnp.int32), axis=-1))

    mine = lax.dynamic_index_in_dim(wanted, col_id, 0, False)
    before = (place[:, None] < place[None, :]).astype(jnp.bfloat16)
    rank = jnp.dot(mine.astype(jnp.bfloat16), before, preferred_element_type=jnp.float32)
    turn = jnp.arange(most, dtype=jnp.int32)
    chosen = mine[:, None, :] & (rank.astype(jnp.int32)[:, None, :] == turn[None, :, None])
    pick = jnp.sum(jnp.where(chosen, place, 0), axis=-1)

    own_rows = lax.dynamic_index_in_dim(rows, col_id, 0, False)
    own_need = lax.dynamic_index_in_dim(need, col_id, 0, False)
    first = row_id * slots
    own_need = lax.dynamic_slice_in_dim(own_need, first, slots, 0)
    target = lax.dynamic_slice_in_dim(own_rows, first, slots, 0)
    panel = lax.dynamic_index_in_dim(kept_tiles, row_id, 0, False)
    panel_rows = panel[:, 0, :].reshape(-1)
    panel_cols = panel[:, 1, :].reshape(-1)
    same = (panel_rows == target[:, None, None]) & (panel_cols == own_rows[None, :, None])
    spot = jnp.arange(n_col * slots, dtype=jnp.int32)
    left = jnp.where(own_need, jnp.sum(jnp.where(same, spot, 0), axis=-1), -1)
    own_chosen = lax.dynamic_index_in_dim(chosen, row_id, 0, False)
    far = jnp.sum(jnp.where(own_chosen[None], left[:, None, :] + 1, 0), axis=-1) - 1
    near = lax.dynamic_slice_in_dim(left, first, slots, 1)
    live = (target >= 0).astype(jnp.int32)
    return largest, pick, jnp.concatenate([near, far], axis=1), live


def local(kept_tiles, density):
    row_id = lax.axis_index("row")
    col_id = lax.axis_index("col")
    n_row, n_col, _, slots = kept_tiles.shape
    tile = density.shape[-1]
    order = n_row * TR * tile
    most = slots * ROW_TILES
    mine = density.reshape(slots, tile, tile)

    def pieces_of(n):
        return jax.ShapeDtypeStruct((n_row, n) + BLOCK, BF16)

    def exchange(x):
        return lax.all_to_all(x, "row", 0, 0, tiled=True)

    def add_over(total, axis, inner, size):
        n = lax.axis_size(axis)

        def moved(i, by):
            place = i // inner % size
            return i + ((place + by) % size - place) * inner

        parts = [lax.ppermute(total, axis, [(i, moved(i, by)) for i in range(n)]) for by in range(1, size)]
        return sum(parts, total)

    first = jax.ShapeDtypeStruct((n_row, slots * BLOCK[0] + EXTRA, BLOCK[1]), BF16)
    (pieces,) = kernel_call(prepare_kernel, [(VMEM, first)], [(VMEM, mine)], touched=4 * mine.size)
    held = exchange(pieces)
    largest, pick, left, live = plan(kept_tiles, row_id, col_id, most)
    pick = jnp.stack([pick // slots * first.shape[1] + pick % slots * BLOCK[0], pick])
    col_live = lax.dynamic_index_in_dim(kept_tiles, col_id, 1, False)[:, 0, :] >= 0
    lanes = jnp.arange(BLOCK[1], dtype=jnp.int32) // PARTS
    mask = sum(((lanes == s) & col_live[:, s:s + 1]).astype(F32) for s in range(slots))

    def finish(capacity, mine, held, mask, pick, left, live):
        left = left[:, :slots + capacity]
        total = VMEM((slots, tile, tile), F32)
        turns = SMEM((capacity + 1,), jnp.int32)
        work = 4 * 2 * tile ** 3
        moved = n_row * capacity * BLOCK[0] * BLOCK[1] * 4
        panel = lax.all_gather(mine, "col", axis=0, tiled=True)
        (sent,) = kernel_call(
            select_first_kernel, [(VMEM, pieces_of(capacity))],
            [(SMEM, pick), (VMEM, held.reshape(-1, BLOCK[1]))], touched=moved,
        )
        (sums,) = kernel_call(
            sum_kernel, [(VMEM, jax.ShapeDtypeStruct((8, BLOCK[1]), F32))], [(VMEM, held), (VMEM, mask)]
        )
        sums = add_over(add_over(sums, "col", 2, n_col // 2), "col", 1, 2)
        received = exchange(sent)
        (square,) = kernel_call(
            functools.partial(first_kernel, order), [(VMEM, pieces_of(slots))],
            [(SMEM, left), (SMEM, live), (pltpu.HBM, pltpu.with_memory_space_constraint(panel, pltpu.HBM)), (VMEM, received),
             (VMEM, mine), (VMEM, sums)],
            scratch=[
                total, turns, VMEM((slots * left.shape[1], tile, tile), BF16),
                pltpu.SemaphoreType.DMA((slots * left.shape[1],)),
            ],
            flops=work, touched=panel.size,
        )
        (sent,) = kernel_call(
            select_kernel, [(VMEM, pieces_of(capacity))], [(SMEM, pick), (VMEM, exchange(square).reshape((-1,) + BLOCK))], touched=moved,
        )
        received = exchange(sent)
        out = jax.ShapeDtypeStruct((slots, tile, tile), BF16)
        return kernel_call(
            functools.partial(second_kernel, order), [(pl.ANY, out), (pl.ANY, out)],
            [(SMEM, left), (SMEM, live), (VMEM, panel), (VMEM, received), (VMEM, square), (VMEM, mine),
             (VMEM, sums)],
            scratch=[total, turns, VMEM(out.shape, BF16), VMEM(out.shape, BF16), pltpu.SemaphoreType.DMA((2 * slots,))],
            flops=work, touched=2 * panel.size,
        )

    capacities = sorted({min(c, most) for c in (5, 6, 7, 8, most)})
    branch = sum((largest > c).astype(jnp.int32) for c in capacities[:-1])
    square, updated = lax.switch(
        branch, [functools.partial(finish, c) for c in capacities],
        mine, held, mask, pick, left, live,
    )
    return square.reshape(density.shape), updated.reshape(density.shape)


def solution(mesh):
    spec = P("row", "col", None, None, None)
    return jax.shard_map(local, mesh=mesh, in_specs=(P(), spec), out_specs=(spec, spec), check_vma=False)
```
